128 devices in a mesh: lat: 8 (over x_hi, z), lon: 16 (over y, x_lo, core).
Axes of the slice: x: 4 (x_hi: 2, x_lo: 2; x = x_hi * 2 + x_lo), y: 4, z: 4, core: 2. Of those that a mesh axis runs over, the one named last changes fastest.
Arguments:
- level_one: bfloat16 [128, 512, 512], P('lat', 'lon'), may hold values from -6 to 6
- gain_attn: float32 [512], replicated, may hold values from 0.5 to 1.5
- w_qkv: bfloat16 [512, 1536], replicated, may hold values from -8 to 8
- w_proj: bfloat16 [512, 512], replicated, may hold values from -0.25 to 0.25
- gain_merge: float32 [2048], replicated, may hold values from 0.5 to 1.5
- w_merge: bfloat16 [2048, 1024], replicated, may hold values from -0.125 to 0.125
- gain_mlp: float32 [1024], replicated, may hold values from 0.5 to 1.5
- w_up: bfloat16 [1024, 4096], P(None, 'lon'), may hold values from -0.1875 to 0.1875
- w_down: bfloat16 [4096, 1024], P('lon'), may hold values from -0.09375 to 0.09375
- cotangent: bfloat16 [64, 256, 1024], P('lat', 'lon'), may hold values from -6 to 6
Outputs:
- level_two: bfloat16 [64, 256, 1024], P('lat', 'lon')
- grad_skip: bfloat16 [128, 512, 512], P('lat', 'lon')
- grad_proj: float32 [512, 512], replicated
- grad_merge: float32 [2048, 1024], P(('lat', 'lon'))
- grad_up: float32 [1024, 4096], P(None, 'lon')
- grad_down: float32 [4096, 1024], P('lon')
The draws below stay inside these ranges and needn't reach their ends.
All inputs are finite; a program needn't handle non-finite values.
Results may differ from the reference program's by a relative error of at most 0.029.
Values may be sent and summed in bfloat16 or wider, within the bound.
No kernel may reach another device: no remote copies, remote signals or barrier semaphores. Data moves between devices by JAX's collectives and lax.ppermute only.
A program may use at most 128 MiB of HBM per device.

```python
import math
import jax
import jax.numpy as jnp
from jax import lax

D1 = 512
D2 = 1024
FF = 4096
HD = 64
WIN = 8
SHIFT = 4
HEADS = 8
NLAT = 128
NLON = 512
NLAT2 = 64
NLON2 = 256


def draw_w_qkv(key, part):
    key = jax.random.fold_in(key, 7)
    base_key = jax.random.fold_in(key, 0)
    base = jax.random.truncated_normal(base_key, -4.0, 4.0, (D1, 3 * D1), jnp.float32) * D1 ** (-0.5)
    return base.astype(jnp.bfloat16)


def shard_levels(rng, extent, cuts, least, high):
    loudness = 1.0
    for position, parts in cuts:
        heights = jax.random.uniform(jax.random.fold_in(jax.random.fold_in(rng, 6), position), (parts,), jnp.float32, least / len(cuts), high / len(cuts))
        loudness = loudness * jnp.repeat(jnp.exp(heights), extent[position] // parts).reshape((-1,) + (1,) * (len(extent) - 1 - position))
    return loudness


def bell_draw(own_key, shape, deviation, bound, cuts=(), dtype=jnp.bfloat16):
    loudness = shard_levels(own_key, shape, cuts, -0.22, 0.18) if cuts else 1.0
    values = jax.random.normal(own_key, shape, jnp.float32) * deviation * loudness
    return jnp.minimum(jnp.maximum(values, -bound), bound).astype(dtype)


def setup_inputs(seed: int = 0) -> dict:
    key_list = jax.random.split(jax.random.key(seed), 11)
    level_one = bell_draw(key_list[0], (NLAT, NLON, D1), 1.0, 6.0, ((0, 8), (1, 16)))
    gain_attn = jnp.clip(1.0 + 0.1 * jax.random.normal(key_list[1], (D1,), jnp.float32), 0.5, 1.5)
    w_qkv = draw_w_qkv(jax.random.fold_in(key_list[10], 71), 0)
    w_proj = bell_draw(key_list[3], (D1, D1), D1 ** -0.5, 0.25)
    gain_merge = jnp.clip(1.0 + 0.1 * jax.random.normal(key_list[4], (4 * D1,), jnp.float32), 0.5, 1.5)
    w_merge = bell_draw(key_list[5], (4 * D1, D2), (4 * D1) ** -0.5, 0.125)
    gain_mlp = jnp.clip(1.0 + 0.1 * jax.random.normal(key_list[6], (D2,), jnp.float32), 0.5, 1.5)
    w_up = bell_draw(key_list[7], (D2, FF), D2 ** -0.5, 0.1875, ((1, 16),))
    w_down = bell_draw(key_list[8], (FF, D2), FF ** -0.5, 0.09375, ((0, 16),))
    cotangent = bell_draw(key_list[9], (NLAT2, NLON2, D2), 1.0, 6.0, ((0, 8), (1, 16)))
    return dict(level_one=level_one, gain_attn=gain_attn, w_qkv=w_qkv, w_proj=w_proj, gain_merge=gain_merge, w_merge=w_merge, gain_mlp=gain_mlp, w_up=w_up, w_down=w_down, cotangent=cotangent)


def layer_norm(values, gain):
    center = values - lax.optimization_barrier(jnp.mean(values, axis=-1, keepdims=True))
    spread = lax.optimization_barrier(jnp.mean(center * center, axis=-1, keepdims=True))
    return center * lax.rsqrt(spread + 1e-05) * gain

def norm_back(values, gain, upstream):
    center = values - lax.optimization_barrier(jnp.mean(values, axis=-1, keepdims=True))
    spread = lax.optimization_barrier(jnp.mean(center * center, axis=-1, keepdims=True))
    factor = lax.rsqrt(spread + 1e-05)
    normal = center * factor
    scaled = upstream * gain
    return factor * (scaled - lax.optimization_barrier(jnp.mean(scaled, axis=-1, keepdims=True)) - normal * lax.optimization_barrier(jnp.mean(scaled * normal, axis=-1, keepdims=True)))

def gelu_tanh(values):
    inner = 0.7978845608 * (values + 0.044715 * values * values * values)
    return 0.5 * values * (1.0 + jnp.tanh(inner))

def gelu_slope(values):
    inner = 0.7978845608 * (values + 0.044715 * values * values * values)
    tangent = jnp.tanh(inner)
    return 0.5 * (1.0 + tangent) + 0.5 * values * (1.0 - tangent * tangent) * 0.7978845608 * (1.0 + 3.0 * 0.044715 * values * values)

def merge_grid(grid):
    lat_len, lon_len, feature = grid.shape
    shaped = grid.reshape(lat_len // 2, 2, lon_len // 2, 2, feature).transpose(0, 2, 3, 1, 4)
    return shaped.reshape(lat_len // 2, lon_len // 2, 4 * feature)

def split_grid(grid):
    lat_half, lon_half, feature = grid.shape
    shaped = grid.reshape(lat_half, lon_half, 2, 2, feature // 4).transpose(0, 3, 1, 2, 4)
    return shaped.reshape(2 * lat_half, 2 * lon_half, feature // 4)

def reference(level_one, gain_attn, w_qkv, w_proj, gain_merge, w_merge, gain_mlp, w_up, w_down, cotangent):
    normed = layer_norm(level_one.astype(jnp.float32), gain_attn).astype(jnp.bfloat16)
    qkv = jnp.dot(normed.reshape(-1, D1), w_qkv, preferred_element_type=jnp.float32).astype(jnp.bfloat16)
    qkv = qkv.reshape(NLAT, NLON, 3 * D1)
    rolled = jnp.roll(qkv, SHIFT, axis=1)
    padded = jnp.pad(rolled, ((SHIFT, WIN - SHIFT), (0, 0), (0, 0)))
    valid_padded = jnp.pad(jnp.ones((NLAT, NLON), jnp.int32), ((SHIFT, WIN - SHIFT), (0, 0)))
    across = NLON // WIN
    bands = (NLAT + WIN) // WIN

    def band(begin_row):
        block = lax.dynamic_slice_in_dim(padded, begin_row, WIN, 0)
        block_ok = lax.dynamic_slice_in_dim(valid_padded, begin_row, WIN, 0)
        block = block.reshape(WIN, across, WIN, 3 * D1).transpose(1, 0, 2, 3).reshape(across, WIN * WIN, 3 * D1)
        block_ok = block_ok.reshape(WIN, across, WIN).transpose(1, 0, 2).reshape(across, WIN * WIN)
        queries = block[:, :, :D1].reshape(across, WIN * WIN, HEADS, HD).astype(jnp.float32)
        keys_win = block[:, :, D1:2 * D1].reshape(across, WIN * WIN, HEADS, HD).astype(jnp.float32)
        values_win = block[:, :, 2 * D1:].reshape(across, WIN * WIN, HEADS, HD).astype(jnp.float32)
        scores = jnp.einsum('wqhd,wkhd->whqk', queries, keys_win) / math.sqrt(HD)
        allowed = block_ok[:, None, None, :] > 0
        scores = jnp.where(allowed, scores, -1e+30)
        highest = lax.optimization_barrier(jnp.max(scores, axis=-1, keepdims=True))
        expo = jnp.exp(scores - highest)
        weights = (expo / lax.optimization_barrier(jnp.sum(expo, axis=-1, keepdims=True))).astype(jnp.bfloat16)
        result = jnp.einsum('whqk,wkhd->wqhd', weights.astype(jnp.float32), values_win).astype(jnp.bfloat16)
        return result.reshape(across, WIN * WIN, D1)
    starts = (jnp.arange(bands) * WIN).astype(jnp.int32)
    outs = lax.map(band, starts)
    outs = outs.reshape(bands, across, WIN, WIN, D1).transpose(0, 2, 1, 3, 4).reshape(bands * WIN, NLON, D1)
    attended = jnp.roll(outs[SHIFT:SHIFT + NLAT], -SHIFT, axis=1)
    flat_att = attended.reshape(-1, D1)
    block_out = (level_one.astype(jnp.float32).reshape(-1, D1) + jnp.dot(flat_att, w_proj, preferred_element_type=jnp.float32)).astype(jnp.bfloat16)
    merged = merge_grid(block_out.reshape(NLAT, NLON, D1)).reshape(-1, 4 * D1)
    merged_norm = layer_norm(merged.astype(jnp.float32), gain_merge).astype(jnp.bfloat16)
    coarse = jnp.dot(merged_norm, w_merge, preferred_element_type=jnp.float32).astype(jnp.bfloat16)
    coarse_norm = layer_norm(coarse.astype(jnp.float32), gain_mlp).astype(jnp.bfloat16)
    pre = jnp.dot(coarse_norm, w_up, preferred_element_type=jnp.float32)
    hidden = gelu_tanh(pre).astype(jnp.bfloat16)
    level_two = (coarse.astype(jnp.float32) + jnp.dot(hidden, w_down, preferred_element_type=jnp.float32)).astype(jnp.bfloat16)
    upstream = cotangent.reshape(-1, D2)
    grad_hidden = jnp.dot(upstream, w_down.T, preferred_element_type=jnp.float32)
    grad_pre = (grad_hidden * gelu_slope(pre)).astype(jnp.bfloat16)
    grad_down = jnp.dot(hidden.T, upstream, preferred_element_type=jnp.float32)
    grad_up = jnp.dot(coarse_norm.T, grad_pre, preferred_element_type=jnp.float32)
    grad_norm = jnp.dot(grad_pre, w_up.T, preferred_element_type=jnp.float32)
    grad_coarse = (upstream.astype(jnp.float32) + norm_back(coarse.astype(jnp.float32), gain_mlp, grad_norm)).astype(jnp.bfloat16)
    grad_merge = jnp.dot(merged_norm.T, grad_coarse, preferred_element_type=jnp.float32)
    grad_mnorm = jnp.dot(grad_coarse, w_merge.T, preferred_element_type=jnp.float32)
    grad_merged = norm_back(merged.astype(jnp.float32), gain_merge, grad_mnorm).astype(jnp.bfloat16)
    grad_skip = split_grid(grad_merged.reshape(NLAT2, NLON2, 4 * D1))
    grad_proj = jnp.dot(flat_att.T, grad_skip.reshape(-1, D1), preferred_element_type=jnp.float32)
    return (level_two.reshape(NLAT2, NLON2, D2), grad_skip, grad_proj, grad_merge, grad_up, grad_down)
```

```python
import math

import jax
import jax.numpy as jnp
from jax import lax
from jax.sharding import Mesh
from jax.sharding import PartitionSpec as P

HD = 64
WIN = 8
SHIFT = 4
LAT = ("xh", "z")
LON = ("y", "xl", "c")


def rotate(value, axis, shift):
    size = lax.axis_size(axis)
    return lax.ppermute(value, axis, [(i, (i + shift) % size) for i in range(size)])


def with_halo(value, sides, width, wrap):
    for axis, dim in sides:
        devices, length = (lax.axis_size(axis), value.shape[dim])
        up = [(i, (i + 1) % devices) for i in range(devices if wrap else devices - 1)]
        down = [(j, i) for i, j in up]
        last = lax.slice_in_dim(value, length - width, length, axis=dim)
        initial = lax.slice_in_dim(value, 0, width, axis=dim)
        before = lax.ppermute(last, axis, up)
        after = lax.ppermute(initial, axis, down)
        value = jnp.concatenate([before, value, after], axis=dim)
    return value


def gather_rel(value, axis):
    size = lax.axis_size(axis)
    return [value] + [rotate(value, axis, k) for k in range(1, size)]


def scatter_rel(parts, axis):
    total = parts[0].astype(jnp.float32)
    for k in range(1, len(parts)):
        total = total + rotate(parts[k].astype(jnp.bfloat16), axis, -k).astype(jnp.float32)
    return total


def scatter_abs(value, axis, dim):
    size, me = lax.axis_size(axis), lax.axis_index(axis)
    total = lax.dynamic_index_in_dim(value, me, dim, keepdims=False).astype(jnp.float32)
    for k in range(1, size):
        piece = lax.dynamic_index_in_dim(value, (me + k) % size, dim, keepdims=False)
        total = total + rotate(piece.astype(jnp.bfloat16), axis, k).astype(jnp.float32)
    return total


def gather_abs(value, axis, dim):
    size, me = lax.axis_size(axis), lax.axis_index(axis)
    shape = value.shape[:dim] + (size,) + value.shape[dim:]
    out = jnp.zeros(shape, value.dtype)
    for k, part in enumerate(gather_rel(value, axis)):
        out = lax.dynamic_update_index_in_dim(out, part, (me - k) % size, dim)
    return out


def layer_norm(values, gain):
    center = values - jnp.mean(values, axis=-1, keepdims=True)
    spread = jnp.mean(center * center, axis=-1, keepdims=True)
    return center * lax.rsqrt(spread + 1e-05) * gain


def norm_back(values, gain, upstream):
    center = values - jnp.mean(values, axis=-1, keepdims=True)
    spread = jnp.mean(center * center, axis=-1, keepdims=True)
    factor = lax.rsqrt(spread + 1e-05)
    normal = center * factor
    scaled = upstream * gain
    return factor * (
        scaled
        - jnp.mean(scaled, axis=-1, keepdims=True)
        - normal * jnp.mean(scaled * normal, axis=-1, keepdims=True)
    )


def gelu_tanh(values):
    inner = 0.7978845608 * (values + 0.044715 * values * values * values)
    return 0.5 * values * (1.0 + jnp.tanh(inner))


def gelu_slope(values):
    inner = 0.7978845608 * (values + 0.044715 * values * values * values)
    tangent = jnp.tanh(inner)
    return 0.5 * (1.0 + tangent) + 0.5 * values * (1.0 - tangent * tangent) * 0.7978845608 * (
        1.0 + 3.0 * 0.044715 * values * values
    )


def merge_grid(grid):
    lat_len, lon_len, feature = grid.shape
    shaped = grid.reshape(lat_len // 2, 2, lon_len // 2, 2, feature).transpose(0, 2, 3, 1, 4)
    return shaped.reshape(lat_len // 2, lon_len // 2, 4 * feature)


def split_grid(grid):
    lat_half, lon_half, feature = grid.shape
    shaped = grid.reshape(lat_half, lon_half, 2, 2, feature // 4).transpose(0, 3, 1, 2, 4)
    return shaped.reshape(2 * lat_half, 2 * lon_half, feature // 4)


def to_windows(grid, lat_windows, lon_windows):
    last = grid.shape[-1]
    shaped = grid.reshape(lat_windows, WIN, lon_windows, WIN, last).transpose(0, 2, 1, 3, 4)
    return shaped.reshape(lat_windows, lon_windows, WIN * WIN, last)


def dot_t(a, b):
    return lax.dot_general(a, b, (((0,), (0,)), ((), ())), preferred_element_type=jnp.float32)


def attend(level_one, gain_attn, w_qkv):
    tile_rows, tile_cols, feature = level_one.shape
    num_heads = feature // HD
    ext_rows = tile_rows + 2 * SHIFT
    ext_cols = tile_cols + 2 * SHIFT
    lat_windows = ext_rows // WIN
    lon_windows = ext_cols // WIN
    fields_cols = with_halo(level_one, ((LON, 1),), SHIFT, True)
    fields_ext = with_halo(fields_cols, ((LAT, 0),), SHIFT, False)
    normed_ext = layer_norm(fields_ext.astype(jnp.float32), gain_attn).astype(jnp.bfloat16)
    qkv_ext = jnp.dot(
        normed_ext.reshape(-1, feature), w_qkv, preferred_element_type=jnp.float32
    ).astype(jnp.bfloat16)
    qkv_ext = qkv_ext.reshape(ext_rows, ext_cols, 3 * feature)
    query_ext = qkv_ext[:, :, :feature]
    pair_ext = qkv_ext[:, :, feature:]
    global_rows = lax.axis_index(LAT) * tile_rows - SHIFT + jnp.arange(ext_rows, dtype=jnp.int32)
    row_valid = ((global_rows >= 0) & (global_rows < tile_rows * lax.axis_size(LAT))).astype(
        jnp.int32
    )
    valid_ext = jnp.broadcast_to(row_valid[:, None], (ext_rows, ext_cols))
    queries = to_windows(query_ext, lat_windows, lon_windows).reshape(
        lat_windows, lon_windows, WIN * WIN, num_heads, HD
    )
    pair_win = to_windows(pair_ext, lat_windows, lon_windows)
    keys_win = pair_win[..., :feature].reshape(lat_windows, lon_windows, WIN * WIN, num_heads, HD)
    values_win = pair_win[..., feature:].reshape(lat_windows, lon_windows, WIN * WIN, num_heads, HD)
    valid_win = to_windows(valid_ext[:, :, None], lat_windows, lon_windows)[..., 0]
    scores = jnp.einsum(
        "abqhd,abkhd->abhqk", queries, keys_win, preferred_element_type=jnp.float32
    ) / math.sqrt(HD)
    allowed = valid_win[:, :, None, None, :] > 0
    scores = jnp.where(allowed, scores, -1e30)
    highest = jnp.max(scores, axis=-1, keepdims=True)
    expo = jnp.exp(scores - highest)
    weights = (expo / jnp.sum(expo, axis=-1, keepdims=True)).astype(jnp.bfloat16)
    result = jnp.einsum(
        "abhqk,abkhd->abqhd", weights, values_win, preferred_element_type=jnp.float32
    ).astype(jnp.bfloat16)
    result = (
        result.reshape(lat_windows, lon_windows, WIN, WIN, feature)
        .transpose(0, 2, 1, 3, 4)
        .reshape(ext_rows, ext_cols, feature)
    )
    return result[SHIFT : SHIFT + tile_rows, SHIFT : SHIFT + tile_cols]


def per_device(
    level_one, gain_attn, w_qkv, w_proj, gain_merge, w_merge, gain_mlp, w_up, w_down, cotangent
):
    tile_rows, tile_cols, feature = level_one.shape
    width = cotangent.shape[-1]
    chunk = w_up.shape[1]
    upstream = cotangent.reshape(-1, width)
    tokens = upstream.shape[0]

    up_x, down_x = rotate(w_up, "xl", 1), rotate(w_down, "xl", 1)
    ups = jnp.concatenate([w_up, rotate(w_up, "c", 1), up_x, rotate(up_x, "c", 1)], axis=1)
    downs = jnp.concatenate(
        [w_down, rotate(w_down, "c", 1), down_x, rotate(down_x, "c", 1)], axis=0
    )
    upstream_band = jnp.concatenate(gather_rel(upstream, "y"), axis=0)

    flat_att = attend(level_one, gain_attn, w_qkv).reshape(-1, feature)
    block_out = (
        level_one.astype(jnp.float32).reshape(-1, feature)
        + jnp.dot(flat_att, w_proj, preferred_element_type=jnp.float32)
    ).astype(jnp.bfloat16)
    merged = merge_grid(block_out.reshape(tile_rows, tile_cols, feature)).reshape(-1, 4 * feature)
    merged_norm = layer_norm(merged.astype(jnp.float32), gain_merge).astype(jnp.bfloat16)
    coarse = jnp.dot(merged_norm, w_merge, preferred_element_type=jnp.float32).astype(jnp.bfloat16)
    coarse_norm = layer_norm(coarse.astype(jnp.float32), gain_mlp).astype(jnp.bfloat16)

    norm_band = jnp.concatenate(gather_rel(coarse_norm, "y"), axis=0)
    pre = jnp.dot(norm_band, ups, preferred_element_type=jnp.float32)
    hidden = gelu_tanh(pre).astype(jnp.bfloat16)
    grad_hidden = jnp.dot(upstream_band, downs.T, preferred_element_type=jnp.float32)
    grad_pre = (grad_hidden * gelu_slope(pre)).astype(jnp.bfloat16)
    norm_part = jnp.dot(grad_pre, ups.T, preferred_element_type=jnp.float32)
    grad_norm = scatter_rel(jnp.split(norm_part, 4), "y")
    grad_coarse = (
        upstream.astype(jnp.float32) + norm_back(coarse.astype(jnp.float32), gain_mlp, grad_norm)
    ).astype(jnp.bfloat16)

    two_part = jnp.dot(hidden, downs, preferred_element_type=jnp.float32)
    summed = scatter_rel(jnp.split(two_part, 4), "y")
    level_two = (coarse.astype(jnp.float32) + summed).astype(jnp.bfloat16)

    both = jnp.stack([dot_t(grad_pre, norm_band), dot_t(hidden, upstream_band)])
    both = both.reshape(2, 4, chunk, width)
    got = rotate(both[:, 1::2].astype(jnp.bfloat16), "c", 1)
    both = both[:, 0::2] + got.astype(jnp.float32)
    got = rotate(both[:, 1].astype(jnp.bfloat16), "xl", 1)
    both = both[:, 0] + got.astype(jnp.float32)
    both = scatter_abs(both.reshape(2, 4, chunk // 4, width), "z", 1)
    both = scatter_abs(both.reshape(2, 2, chunk // 8, width), "xh", 1)
    both = gather_abs(both.astype(jnp.bfloat16), "xh", 1).reshape(2, chunk // 4, width)
    both = gather_abs(both, "z", 1).reshape(2, chunk, width)
    grad_up = both[0].T.astype(jnp.float32)
    grad_down = both[1].astype(jnp.float32)

    grad_mnorm = jnp.dot(grad_coarse, w_merge.T, preferred_element_type=jnp.float32)
    grad_merged = norm_back(merged.astype(jnp.float32), gain_merge, grad_mnorm).astype(jnp.bfloat16)
    grad_skip = split_grid(grad_merged.reshape(tile_rows // 2, tile_cols // 2, 4 * feature))
    proj_term = dot_t(flat_att, grad_skip.reshape(-1, feature))

    me = lax.axis_index("y")
    pieces = merged_norm.reshape(tokens, 8, 4, 64)
    mine = [lax.dynamic_index_in_dim(pieces, me, 2, keepdims=False)]
    for k in range(1, 4):
        piece = lax.dynamic_index_in_dim(pieces, (me + k) % 4, 2, keepdims=False)
        mine.append(rotate(piece.reshape(tokens, 512), "y", k).reshape(tokens, 8, 64))
    mine = jnp.concatenate(mine, axis=0).reshape(4 * tokens, 512)
    coarse_band = jnp.concatenate(gather_rel(grad_coarse, "y"), axis=0)
    merge_term = dot_t(mine, coarse_band)
    term = jnp.concatenate([merge_term, proj_term], axis=1)
    last = term.shape[1]
    term = scatter_abs(term.reshape(8, 2, 2, 16, last), "c", 2)
    term = scatter_abs(term, "xl", 1)
    term = scatter_abs(term.reshape(2, 4, 16, last), "z", 1)
    term = scatter_abs(term, "xh", 0)
    grad_merge = term[:, :width]
    proj = sum(p.astype(jnp.float32) for p in gather_rel(term[:, width:].astype(jnp.bfloat16), "y"))
    proj = gather_abs(proj.astype(jnp.bfloat16), "xh", 0)
    proj = gather_abs(proj, "z", 1)
    proj = gather_abs(proj.reshape(8, 16, feature), "xl", 1)
    proj = gather_abs(proj, "c", 2)
    grad_proj = proj.reshape(feature, feature).astype(jnp.float32)

    level_two = level_two.reshape(tile_rows // 2, tile_cols // 2, width)
    return (level_two, grad_skip, grad_proj, grad_merge, grad_up, grad_down)


def solution(mesh):
    fine = Mesh(mesh.devices.reshape(2, 4, 4, 2, 2), LAT + LON)
    grid = P(LAT, LON, None)
    placed = (grid, P(), P(), P(), P(), P(), P(), P(None, LON), P(LON, None), grid)
    return jax.shard_map(
        per_device,
        mesh=fine,
        in_specs=placed,
        out_specs=(grid, grid, P(), P(LAT + LON, None), P(None, LON), P(LON, None)),
        check_vma=False,
    )
```

```python
import jax
import jax.numpy as jnp
from jax import lax
from jax.experimental import pallas as pl
from jax.experimental.pallas import tpu as pltpu
from jax.sharding import Mesh
from jax.sharding import PartitionSpec as P

HD = 64
WIN = 8
SHIFT = 4
LAT = ("xh", "z")
LON = ("y", "xl", "c")
F32 = jnp.float32
BF = jnp.bfloat16
VMEM = pl.BlockSpec(memory_space=pltpu.VMEM)
SMEM = pl.BlockSpec(memory_space=pltpu.SMEM)


def rotate(value, axis, shift):
    size = lax.axis_size(axis)
    return lax.ppermute(value, axis, [(i, (i + shift) % size) for i in range(size)])


def params():
    return pltpu.CompilerParams(vmem_limit_bytes=48 * 2**20)


def cost(flops, size, special=0):
    return pl.CostEstimate(flops=flops, bytes_accessed=size, transcendentals=special)


def scatter_rel(parts, axis, way):
    total = parts[0].astype(F32)
    for k in range(1, len(parts)):
        total = total + rotate(parts[k], axis, way * k).astype(F32)
    return total


def gather_rel(value, axis):
    return [value] + [rotate(value, axis, k) for k in range(1, lax.axis_size(axis))]


def normalise(values, gain):
    center = values - jnp.mean(values, axis=-1, keepdims=True)
    spread = jnp.mean(center * center, axis=-1, keepdims=True)
    return center * lax.rsqrt(spread + 1e-05) * gain


def nt(a, b):
    return lax.dot_general(a, b, (((1,), (1,)), ((), ())), preferred_element_type=F32)


def tn(a, b):
    return lax.dot_general(a, b, (((0,), (0,)), ((), ())), preferred_element_type=F32)


def attend_kernel(
    place_ref, own_ref, top_ref, bottom_ref, left_ref, right_ref, gain_attn_ref, qkv_ref, proj_ref,
    gain_merge_ref, merge_ref, gain_mlp_ref,
    norm_out, coarse_out, merged_out, pick_out, att_out,
    field, att, hold,
):
    rows, cols, width = own_ref.shape
    lanes = width // 128
    for n in range(lanes):
        part = slice(n * 128, (n + 1) * 128)
        field[n, SHIFT : SHIFT + rows, SHIFT : SHIFT + cols, :] = own_ref[:, :, part].astype(F32)
        field[n, :SHIFT, SHIFT : SHIFT + cols, :] = top_ref[:, :, part].astype(F32)
        field[n, SHIFT + rows :, SHIFT : SHIFT + cols, :] = bottom_ref[:, :, part].astype(F32)
        field[n, :, :SHIFT, :] = left_ref[:, :, part].astype(F32)
        field[n, :, SHIFT + cols :, :] = right_ref[:, :, part].astype(F32)
    across = (cols + WIN) // WIN
    size = WIN * WIN
    low = lax.broadcasted_iota(jnp.int32, (size, 128), 1) < HD
    key_row = lax.broadcasted_iota(jnp.int32, (2 * size, size), 1) // WIN
    first = place_ref[0] * rows - SHIFT
    total = place_ref[1] * rows

    def band(a, carry):
        for b in range(across):
            x = jnp.concatenate(
                [
                    field[n, pl.ds(a * WIN, WIN), b * WIN : (b + 1) * WIN, :].reshape(size, 128)
                    for n in range(lanes)
                ],
                axis=1,
            )
            hold[b * size : (b + 1) * size, :] = normalise(x, gain_attn_ref[...]).astype(BF)
        qkv = jnp.dot(hold[...], qkv_ref[...], preferred_element_type=F32).astype(BF)
        row = first + a * WIN + key_row
        allowed = (row >= 0) & (row < total)
        for b in range(across):
            here = slice(b * size, (b + 1) * size)
            for p in range(lanes):
                q = qkv[here, p * 128 : (p + 1) * 128]
                k = qkv[here, width + p * 128 : width + (p + 1) * 128]
                v = qkv[here, 2 * width + p * 128 : 2 * width + (p + 1) * 128]
                none = jnp.zeros_like(q)
                pair = jnp.concatenate([jnp.where(low, q, none), jnp.where(low, none, q)], axis=0)
                scores = jnp.where(allowed, nt(pair, k) * (1.0 / 8.0), -1e30)
                expo = jnp.exp(scores - jnp.max(scores, axis=1, keepdims=True))
                weights = (expo / jnp.sum(expo, axis=1, keepdims=True)).astype(BF)
                both = jnp.dot(weights, v, preferred_element_type=F32)
                out = jnp.where(low, both[:size], both[size:]).astype(BF).astype(F32)
                att[p, pl.ds(a * WIN, WIN), b * WIN : (b + 1) * WIN, :] = out.reshape(WIN, WIN, 128)
        return carry

    lax.fori_loop(0, (rows + WIN) // WIN, band, 0)

    half_rows, half_cols = rows // 2, cols // 2
    tokens = half_rows * half_cols
    pieces = []
    for p in range(4):
        di, dj = p % 2, p // 2
        def pick(ref):
            return jnp.concatenate(
                [
                    jnp.concatenate(
                        [
                            ref[n, SHIFT + di + 2 * i, pl.ds(SHIFT + dj, half_cols, stride=2), :]
                            for i in range(half_rows)
                        ],
                        axis=0,
                    )
                    for n in range(lanes)
                ],
                axis=1,
            )
        got = pick(att).astype(BF)
        att_out[:, p * width : (p + 1) * width] = got
        block = pick(field) + jnp.dot(got, proj_ref[...], preferred_element_type=F32)
        block = block.astype(BF)
        merged_out[:, p * width : (p + 1) * width] = block
    merged = merged_out[...].astype(F32)
    merged_norm = normalise(merged, gain_merge_ref[...]).astype(BF)
    for n in range(4):
        pick_out[lax.rem(n + 4 - place_ref[2], 4)] = jnp.concatenate(
            [merged_norm[:, g * 256 + n * 64 : g * 256 + (n + 1) * 64] for g in range(8)], axis=1
        )
    coarse = jnp.dot(merged_norm, merge_ref[...], preferred_element_type=F32).astype(BF)
    coarse_out[...] = coarse
    norm_out[...] = normalise(coarse.astype(F32), gain_mlp_ref[...]).astype(BF)


def attend(place, own, top, bottom, left, right, gain_attn, w_qkv, w_proj, gain_merge, w_merge, gain_mlp):
    rows, cols, width = own.shape
    tokens = rows * cols // 4
    wide = w_merge.shape[1]
    shapes = [
        jax.ShapeDtypeStruct((tokens, wide), BF),
        jax.ShapeDtypeStruct((tokens, wide), BF),
        jax.ShapeDtypeStruct((tokens, 4 * width), BF),
        jax.ShapeDtypeStruct((4, tokens, width), BF),
        jax.ShapeDtypeStruct((tokens, 4 * width), BF),
    ]
    return pl.pallas_call(
        attend_kernel,
        out_shape=shapes,
        in_specs=[SMEM] + [VMEM] * 11,
        out_specs=[VMEM] * 5,
        scratch_shapes=[
            pltpu.VMEM((width // 128, rows + WIN, cols + WIN, 128), F32),
            pltpu.VMEM((width // 128, rows + WIN, cols + WIN, 128), F32),
            pltpu.VMEM(((cols + WIN) * WIN, width), BF),
        ],
        compiler_params=params(),
        cost_estimate=cost(4 * 10**9, 12 * 2**20, 10**6),
    )(place, own, top, bottom, left, right, gain_attn.reshape(1, -1), w_qkv, w_proj, gain_merge.reshape(1, -1), w_merge, gain_mlp.reshape(1, -1))


def hidden_kernel(*refs):
    norms, ups, downs = refs[0:4], refs[8:12], refs[12:16]
    streams = refs[4:8]
    parts = refs[16:20]
    hidden_out, pre_out, norm_all, stream_all, total = refs[20:]
    tokens = norms[0].shape[0]
    chunk = ups[0].shape[1]
    for t in range(4):
        norm_all[t * tokens : (t + 1) * tokens, :] = norms[t][...]
        stream_all[t * tokens : (t + 1) * tokens, :] = streams[t][...]
    for m in range(4):
        up = ups[m][...]
        pre = jnp.dot(norm_all[...], up, preferred_element_type=F32)
        grad_hidden = nt(stream_all[...], downs[m][...])
        tangent = jnp.tanh(0.7978845608 * (pre + 0.044715 * pre * pre * pre))
        hidden = 0.5 * pre * (1.0 + tangent)
        slope = 0.5 * (1.0 + tangent) + 0.5 * pre * (1.0 - tangent * tangent) * 0.7978845608 * (
            1.0 + 3.0 * 0.044715 * pre * pre
        )
        here = slice(m * chunk, (m + 1) * chunk)
        hidden_out[:, here] = hidden.astype(BF)
        grad_pre = (grad_hidden * slope).astype(BF)
        pre_out[:, here] = grad_pre
        part = nt(grad_pre, up)
        if m == 0:
            total[...] = part
        elif m < 3:
            total[...] += part
        else:
            for t in range(4):
                rows = slice(t * tokens, (t + 1) * tokens)
                parts[t][...] = (total[rows, :] + part[rows, :]).astype(BF)


def hidden_units(norms, streams, ups, downs):
    tokens, width = norms[0].shape
    chunk = ups[0].shape[1]
    out = [jax.ShapeDtypeStruct((tokens, width), BF)] * 4
    out += [jax.ShapeDtypeStruct((4 * tokens, 4 * chunk), BF)] * 2
    return pl.pallas_call(
        hidden_kernel,
        out_shape=out,
        in_specs=[VMEM] * 16,
        out_specs=[VMEM] * 6,
        scratch_shapes=[
            pltpu.VMEM((4 * tokens, width), BF),
            pltpu.VMEM((4 * tokens, width), BF),
            pltpu.VMEM((4 * tokens, width), F32),
        ],
        compiler_params=params(),
        cost_estimate=cost(4 * 10**9, 10 * 2**20, 10**6),
    )(*norms, *streams, *ups, *downs)


def weight_grad_kernel(*refs):
    place = refs[0]
    norms, streams = refs[1:5], refs[5:9]
    hidden, pre, send, keep, norm_all, stream_all = refs[9:]
    tokens = norms[0].shape[0]
    chunk = send.shape[3]
    for t in range(4):
        norm_all[t * tokens : (t + 1) * tokens, :] = norms[t][...]
        stream_all[t * tokens : (t + 1) * tokens, :] = streams[t][...]
    for m in (1, 3, 0, 2):
        here = slice(m * chunk, (m + 1) * chunk)
        up = tn(norm_all[...], pre[:, here])
        down = tn(hidden[:, here], stream_all[...])
        target = send if m % 2 else keep
        for n in range(4):
            slot = lax.rem(n + 4 - place[3], 4)
            block = slice(n * 256, (n + 1) * 256)
            target[0, m // 2, slot] = up[block, :].astype(target.dtype)
            target[1, m // 2, slot] = down[:, block].astype(target.dtype)


def weight_grads(place, norms, streams, hidden, pre):
    tokens, width = norms[0].shape
    chunk = pre.shape[1] // 4
    shape = (2, 2, 4, chunk, width // 4)
    return pl.pallas_call(
        weight_grad_kernel,
        out_shape=[jax.ShapeDtypeStruct(shape, BF), jax.ShapeDtypeStruct(shape, F32)],
        in_specs=[SMEM] + [VMEM] * 10,
        out_specs=[VMEM] * 2,
        scratch_shapes=[pltpu.VMEM((4 * tokens, width), BF), pltpu.VMEM((4 * tokens, width), BF)],
        compiler_params=params(),
        cost_estimate=cost(4 * 10**9, 12 * 2**20),
    )(place, *norms, *streams, hidden, pre)


def down_kernel(*refs):
    hidden, downs, parts = refs[0], refs[1:5], refs[5:9]
    tokens = parts[0].shape[0]
    chunk = downs[0].shape[0]
    for t in range(4):
        rows = slice(t * tokens, (t + 1) * tokens)
        total = jnp.dot(hidden[rows, :chunk], downs[0][...], preferred_element_type=F32)
        for m in range(1, 4):
            total += jnp.dot(
                hidden[rows, m * chunk : (m + 1) * chunk],
                downs[m][...],
                preferred_element_type=F32,
            )
        parts[t][...] = total.astype(BF)


def down_parts(hidden, downs):
    tokens = hidden.shape[0] // 4
    return pl.pallas_call(
        down_kernel,
        out_shape=[jax.ShapeDtypeStruct((tokens, downs[0].shape[1]), BF)] * 4,
        in_specs=[VMEM] * 5,
        out_specs=[VMEM] * 4,
        compiler_params=params(),
        cost_estimate=cost(10**9, 4 * 2**20),
    )(hidden, *downs)


def merge_grad_kernel(*refs):
    place = refs[0]
    lefts, rights = refs[1:5], refs[5:9]
    send, keep, left_all, right_all, blocks = refs[9:]
    tokens, width = lefts[0].shape
    for t in range(4):
        left_all[t * tokens : (t + 1) * tokens, :] = lefts[t][...]
        right_all[t * tokens : (t + 1) * tokens, :] = rights[t][...]
    part = tn(left_all[...], right_all[...])
    for n in range(width // 16):
        dc = lax.rem(n % 2 + place[5], 2)
        dx = lax.rem(n // 2 % 2 + place[4], 2)
        dz = lax.rem(n // 4 % 4 + 4 - place[3], 4)
        dh = lax.rem(n // 16 + place[6], 2)
        blocks[dc, dx, dz, dh] = part[n * 16 : (n + 1) * 16, :]
    keep[...] = blocks[0]
    send[...] = blocks[1].astype(BF)


def merge_grads(place, lefts, rights):
    tokens, width = lefts[0].shape
    last = rights[0].shape[1]
    shape = (2, 4, 2, 16, last)
    return pl.pallas_call(
        merge_grad_kernel,
        out_shape=[jax.ShapeDtypeStruct(shape, BF), jax.ShapeDtypeStruct(shape, F32)],
        in_specs=[SMEM] + [VMEM] * 8,
        out_specs=[VMEM] * 2,
        scratch_shapes=[
            pltpu.VMEM((4 * tokens, width), BF),
            pltpu.VMEM((4 * tokens, last), BF),
            pltpu.VMEM((2,) + shape, F32),
        ],
        compiler_params=params(),
        cost_estimate=cost(10**9, 6 * 2**20),
    )(place, *lefts, *rights)


def place_kernel(*refs):
    place, parts, up, down = refs[0], refs[1:5], refs[5], refs[6]
    for k in range(4):
        start = pl.multiple_of(lax.rem(place[3] + 4 - k, 4) * 256, 256)
        up[pl.ds(start, 256), :] = parts[k][0].astype(F32)
        down[:, pl.ds(start, 256)] = parts[k][1].astype(F32)


def place_blocks(place, parts):
    chunk = parts[0].shape[1]
    return pl.pallas_call(
        place_kernel,
        out_shape=[
            jax.ShapeDtypeStruct((4 * 256, chunk), F32),
            jax.ShapeDtypeStruct((chunk, 4 * 256), F32),
        ],
        in_specs=[SMEM] + [VMEM] * 4,
        out_specs=[VMEM] * 2,
        compiler_params=params(),
        cost_estimate=cost(10**6, 3 * 2**20),
    )(place, *parts)


def norm_back(values, gain, upstream):
    center = values - jnp.mean(values, axis=-1, keepdims=True)
    spread = jnp.mean(center * center, axis=-1, keepdims=True)
    factor = lax.rsqrt(spread + 1e-05)
    normal = center * factor
    scaled = upstream * gain
    return factor * (
        scaled
        - jnp.mean(scaled, axis=-1, keepdims=True)
        - normal * jnp.mean(scaled * normal, axis=-1, keepdims=True)
    )


def skip_kernel(coarse_grad, gain, merge, merged, att, skip, proj, hold):
    lanes = hold.shape[0]
    width = lanes * 128
    half_rows, half_cols = hold.shape[1] // 2, hold.shape[2] // 2
    grad = nt(coarse_grad[...], merge[...])
    grad = norm_back(merged[...].astype(F32), gain[...], grad).astype(BF)
    total = None
    for p in range(4):
        di, dj = p % 2, p // 2
        piece = grad[:, p * width : (p + 1) * width]
        part = tn(att[:, p * width : (p + 1) * width], piece)
        total = part if total is None else total + part
        wide = piece.astype(F32)
        for n in range(lanes):
            for i in range(half_rows):
                hold[n, di + 2 * i, pl.ds(dj, half_cols, stride=2), :] = wide[
                    i * half_cols : (i + 1) * half_cols, n * 128 : (n + 1) * 128
                ]
    for n in range(lanes):
        skip[:, :, n * 128 : (n + 1) * 128] = hold[n].astype(BF)
        proj[n] = total[:, n * 128 : (n + 1) * 128].reshape(width // 16, 16, 128).astype(BF)


def skip_grads(coarse_grad, gain, merge, merged, att, rows, cols):
    width = att.shape[1] // 4
    return pl.pallas_call(
        skip_kernel,
        out_shape=[
            jax.ShapeDtypeStruct((rows, cols, width), BF),
            jax.ShapeDtypeStruct((width // 128, width // 16, 16, 128), BF),
        ],
        in_specs=[VMEM] * 5,
        out_specs=[VMEM] * 2,
        scratch_shapes=[pltpu.VMEM((width // 128, rows, cols, 128), F32)],
        compiler_params=params(),
        cost_estimate=cost(10**9, 8 * 2**20),
    )(coarse_grad, gain.reshape(1, -1), merge, merged, att)


def per_device(
    level_one, gain_attn, w_qkv, w_proj, gain_merge, w_merge, gain_mlp, w_up, w_down, cotangent
):
    tile_rows, tile_cols, feature = level_one.shape
    width = cotangent.shape[-1]
    upstream = cotangent.reshape(-1, width)
    place = jnp.stack(
        [lax.axis_index(LAT), jnp.int32(lax.axis_size(LAT))]
        + [lax.axis_index(name) for name in ("y", "z", "xl", "c", "xh")]
    ).astype(jnp.int32)

    top = rotate(level_one[-SHIFT:], LAT, 1)
    bottom = rotate(level_one[:SHIFT], LAT, -1)
    tall = [top, level_one, bottom]
    left = rotate(jnp.concatenate([part[:, -SHIFT:] for part in tall], axis=0), LON, 1)
    right = rotate(jnp.concatenate([part[:, :SHIFT] for part in tall], axis=0), LON, -1)

    left, right, first_up, first_down, first_stream = lax.optimization_barrier(
        (left, right, w_up, w_down, upstream)
    )
    up_x, down_x = rotate(first_up, "xl", 1), rotate(first_down, "xl", 1)
    ups = [w_up, rotate(first_up, "c", 1), up_x, rotate(up_x, "c", 1)]
    downs = [w_down, rotate(first_down, "c", 1), down_x, rotate(down_x, "c", 1)]
    streams = gather_rel(first_stream, "y")

    coarse_norm, coarse, merged, picks, att = attend(
        place, level_one, top, bottom, left, right, gain_attn, w_qkv, w_proj,
        gain_merge, w_merge, gain_mlp,
    )
    norms = gather_rel(coarse_norm, "y")
    *norm_parts, hidden, grad_pre = hidden_units(norms, streams, ups, downs)
    grad_norm = scatter_rel(norm_parts, "y", -1)
    grad_coarse = (
        upstream.astype(F32) + norm_back(coarse.astype(F32), gain_mlp, grad_norm)
    ).astype(BF)

    send, keep = weight_grads(place, norms, streams, hidden, grad_pre)
    keep = keep + rotate(send, "c", 1).astype(F32)
    up = keep[0, 0] + rotate(keep[0, 1].astype(BF), "xl", 1).astype(F32)
    up = scatter_rel([up[0]] + [up[k].astype(BF) for k in range(1, 4)], "z", 1)
    down = scatter_rel([keep[1, :, 0]] + [keep[1, :, k].astype(BF) for k in range(1, 4)], "z", 1)
    down = down[0] + rotate(down[1].astype(BF), "xl", 1).astype(F32)
    both = jnp.stack([up, down]).astype(BF)
    both = (both.astype(F32) + rotate(both, "xh", 1).astype(F32)).astype(BF)
    grad_up, grad_down = place_blocks(place, gather_rel(both, "z"))

    parts = down_parts(hidden, downs)
    level_two = (coarse.astype(F32) + scatter_rel(parts, "y", -1)).astype(BF)

    grad_skip, proj_part = skip_grads(
        grad_coarse, gain_merge, w_merge, merged, att, tile_rows, tile_cols
    )

    lefts = [picks[0]] + [rotate(picks[k], "y", k) for k in range(1, 4)]
    rights = gather_rel(grad_coarse, "y")
    send, keep = merge_grads(place, lefts, rights)
    keep = keep + rotate(send, "c", 1).astype(F32)
    keep = keep[0] + rotate(keep[1].astype(BF), "xl", 1).astype(F32)
    keep = scatter_rel([keep[0]] + [keep[k].astype(BF) for k in range(1, 4)], "z", 1)
    grad_merge = keep[0] + rotate(keep[1].astype(BF), "xh", 1).astype(F32)

    every = LAT + LON
    blocks = proj_part.reshape((128,) + proj_part.shape[2:])
    blocks = lax.all_to_all(blocks, every, 0, 0)
    block = jnp.sum(blocks.astype(F32), axis=0).astype(BF)
    blocks = lax.all_to_all(jnp.broadcast_to(block, blocks.shape), every, 0, 0)
    grad_proj = blocks.reshape(proj_part.shape).transpose(1, 2, 0, 3).reshape(feature, feature)
    grad_proj = grad_proj.astype(F32)

    level_two = level_two.reshape(tile_rows // 2, tile_cols // 2, width)
    return (level_two, grad_skip, grad_proj, grad_merge, grad_up, grad_down)


def solution(mesh):
    fine = Mesh(mesh.devices.reshape(2, 4, 4, 2, 2), LAT + LON)
    grid = P(LAT, LON, None)
    placed = (grid, P(), P(), P(), P(), P(), P(), P(None, LON), P(LON, None), grid)
    return jax.shard_map(
        per_device,
        mesh=fine,
        in_specs=placed,
        out_specs=(grid, grid, P(), P(LAT + LON, None), P(None, LON), P(LON, None)),
        check_vma=False,
    )
```

```python
import jax
import jax.numpy as jnp
from jax import lax
from jax.experimental import pallas as pl
from jax.experimental.pallas import tpu as pltpu
from jax.sharding import Mesh
from jax.sharding import PartitionSpec as P

HD = 64
WIN = 8
SHIFT = 4
LAT = ("xh", "z")
LON = ("y", "xl", "c")
F32 = jnp.float32
BF = jnp.bfloat16
VMEM = pl.BlockSpec(memory_space=pltpu.VMEM)
SMEM = pl.BlockSpec(memory_space=pltpu.SMEM)


def rotate(value, axis, shift):
    size = lax.axis_size(axis)
    return lax.ppermute(value, axis, [(i, (i + shift) % size) for i in range(size)])


def params():
    return pltpu.CompilerParams(vmem_limit_bytes=62 * 2**20)


def cost():
    return pl.CostEstimate(flops=1000, bytes_accessed=1000, transcendentals=0)


def together(*values):
    return lax.optimization_barrier(values)


def scatter_rel(parts, axis, way):
    total = parts[0].astype(F32)
    for k in range(1, len(parts)):
        total = total + rotate(parts[k], axis, way * k).astype(F32)
    return total


def gather_rel(value, axis):
    return [value] + [rotate(value, axis, k) for k in range(1, lax.axis_size(axis))]


def normalise(values, gain):
    center = values - jnp.mean(values, axis=-1, keepdims=True)
    spread = jnp.mean(center * center, axis=-1, keepdims=True)
    return center * lax.rsqrt(spread + 1e-05) * gain


def nt(a, b):
    return lax.dot_general(a, b, (((1,), (1,)), ((), ())), preferred_element_type=F32)


def tn(a, b):
    return lax.dot_general(a, b, (((0,), (0,)), ((), ())), preferred_element_type=F32)


def attend_kernel(
    place_ref, own_ref, top_ref, bottom_ref, left_ref, right_ref, gain_attn_ref, qkv_ref, proj_ref,
    gain_merge_ref, merge_ref, gain_mlp_ref,
    norm_out, coarse_out, merged_out, pick_out, att_out,
    field, att, hold,
):
    rows, cols, width = own_ref.shape
    lanes = width // 128
    for n in range(lanes):
        part = slice(n * 128, (n + 1) * 128)
        field[n, SHIFT : SHIFT + rows, SHIFT : SHIFT + cols, :] = own_ref[:, :, part].astype(F32)
        field[n, :SHIFT, SHIFT : SHIFT + cols, :] = top_ref[:, :, part].astype(F32)
        field[n, SHIFT + rows :, SHIFT : SHIFT + cols, :] = bottom_ref[:, :, part].astype(F32)
        field[n, :, :SHIFT, :] = left_ref[:, :, part].astype(F32)
        field[n, :, SHIFT + cols :, :] = right_ref[:, :, part].astype(F32)
    across = (cols + WIN) // WIN
    size = WIN * WIN
    low = lax.broadcasted_iota(jnp.int32, (size, 128), 1) < HD
    key_row = lax.broadcasted_iota(jnp.int32, (2 * size, size), 1) // WIN
    first = place_ref[0] * rows - SHIFT
    total = place_ref[1] * rows

    def band(a, carry):
        for b in range(across):
            x = jnp.concatenate(
                [
                    field[n, pl.ds(a * WIN, WIN), b * WIN : (b + 1) * WIN, :].reshape(size, 128)
                    for n in range(lanes)
                ],
                axis=1,
            )
            hold[b * size : (b + 1) * size, :] = normalise(x, gain_attn_ref[...]).astype(BF)
        qkv = jnp.dot(hold[...], qkv_ref[...], preferred_element_type=F32).astype(BF)
        row = first + a * WIN + key_row
        allowed = (row >= 0) & (row < total)
        for b in range(across):
            here = slice(b * size, (b + 1) * size)
            for p in range(lanes):
                q = qkv[here, p * 128 : (p + 1) * 128]
                k = qkv[here, width + p * 128 : width + (p + 1) * 128]
                v = qkv[here, 2 * width + p * 128 : 2 * width + (p + 1) * 128]
                none = jnp.zeros_like(q)
                pair = jnp.concatenate([jnp.where(low, q, none), jnp.where(low, none, q)], axis=0)
                scores = jnp.where(allowed, nt(pair, k) * (1.0 / 8.0), -1e30)
                expo = jnp.exp(scores - jnp.max(scores, axis=1, keepdims=True))
                weights = (expo / jnp.sum(expo, axis=1, keepdims=True)).astype(BF)
                both = jnp.dot(weights, v, preferred_element_type=F32)
                out = jnp.where(low, both[:size], both[size:]).astype(BF).astype(F32)
                att[p, pl.ds(a * WIN, WIN), b * WIN : (b + 1) * WIN, :] = out.reshape(WIN, WIN, 128)
        return carry

    lax.fori_loop(0, (rows + WIN) // WIN, band, 0)

    half_rows, half_cols = rows // 2, cols // 2
    tokens = half_rows * half_cols
    pieces = []
    for p in range(4):
        di, dj = p % 2, p // 2
        def pick(ref):
            return jnp.concatenate(
                [
                    jnp.concatenate(
                        [
                            ref[n, SHIFT + di + 2 * i, pl.ds(SHIFT + dj, half_cols, stride=2), :]
                            for i in range(half_rows)
                        ],
                        axis=0,
                    )
                    for n in range(lanes)
                ],
                axis=1,
            )
        got = pick(att).astype(BF)
        att_out[:, p * width : (p + 1) * width] = got
        block = pick(field) + jnp.dot(got, proj_ref[...], preferred_element_type=F32)
        block = block.astype(BF)
        merged_out[:, p * width : (p + 1) * width] = block
    merged = merged_out[...].astype(F32)
    merged_norm = normalise(merged, gain_merge_ref[...]).astype(BF)
    for n in range(4):
        pick_out[n] = jnp.concatenate(
            [merged_norm[:, g * 256 + n * 64 : g * 256 + (n + 1) * 64] for g in range(8)], axis=1
        )
    coarse = jnp.dot(merged_norm, merge_ref[...], preferred_element_type=F32).astype(BF)
    coarse_out[...] = coarse
    norm_out[...] = normalise(coarse.astype(F32), gain_mlp_ref[...]).astype(BF)


def attend(place, own, top, bottom, left, right, gain_attn, w_qkv, w_proj, gain_merge, w_merge, gain_mlp):
    rows, cols, width = own.shape
    tokens = rows * cols // 4
    wide = w_merge.shape[1]
    shapes = [
        jax.ShapeDtypeStruct((tokens, wide), BF),
        jax.ShapeDtypeStruct((tokens, wide), BF),
        jax.ShapeDtypeStruct((tokens, 4 * width), BF),
        jax.ShapeDtypeStruct((4, tokens, width), BF),
        jax.ShapeDtypeStruct((tokens, 4 * width), BF),
    ]
    return pl.pallas_call(
        attend_kernel,
        out_shape=shapes,
        in_specs=[SMEM] + [VMEM] * 11,
        out_specs=[VMEM] * 5,
        scratch_shapes=[
            pltpu.VMEM((width // 128, rows + WIN, cols + WIN, 128), F32),
            pltpu.VMEM((width // 128, rows + WIN, cols + WIN, 128), F32),
            pltpu.VMEM(((cols + WIN) * WIN, width), BF),
        ],
        compiler_params=params(),
        cost_estimate=cost(),
    )(place, own, top, bottom, left, right, gain_attn.reshape(1, -1), w_qkv, w_proj, gain_merge.reshape(1, -1), w_merge, gain_mlp.reshape(1, -1))


def hidden_kernel(*refs):
    norms, streams, ups, downs, parts = (refs[i : i + 4] for i in range(0, 20, 4))
    hidden_out, pre_out, norm_all, stream_all, total = refs[20:]
    tokens = norms[0].shape[0]
    chunk = ups[0].shape[1]
    for t in range(4):
        norm_all[t * tokens : (t + 1) * tokens, :] = norms[t][...]
        stream_all[t * tokens : (t + 1) * tokens, :] = streams[t][...]
    for m in range(4):
        up = ups[m][...]
        pre = jnp.dot(norm_all[...], up, preferred_element_type=F32)
        grad_hidden = nt(stream_all[...], downs[m][...])
        tangent = jnp.tanh(0.7978845608 * (pre + 0.044715 * pre * pre * pre))
        hidden = 0.5 * pre * (1.0 + tangent)
        slope = 0.5 * (1.0 + tangent) + 0.5 * pre * (1.0 - tangent * tangent) * 0.7978845608 * (
            1.0 + 3.0 * 0.044715 * pre * pre
        )
        here = slice(m * chunk, (m + 1) * chunk)
        hidden_out[:, here] = hidden.astype(BF)
        grad_pre = (grad_hidden * slope).astype(BF)
        pre_out[:, here] = grad_pre
        part = nt(grad_pre, up)
        if m == 0:
            total[...] = part
        elif m < 3:
            total[...] += part
        else:
            for t in range(4):
                rows = slice(t * tokens, (t + 1) * tokens)
                parts[t][...] = (total[rows, :] + part[rows, :]).astype(BF)


def hidden_units(norms, streams, ups, downs):
    tokens, width = norms[0].shape
    chunk = ups[0].shape[1]
    out = [jax.ShapeDtypeStruct((tokens, width), BF)] * 4
    out += [jax.ShapeDtypeStruct((4 * tokens, 4 * chunk), BF)] * 2
    return pl.pallas_call(
        hidden_kernel,
        out_shape=out,
        in_specs=[VMEM] * 16,
        out_specs=[VMEM] * 6,
        scratch_shapes=[
            pltpu.VMEM((4 * tokens, width), BF),
            pltpu.VMEM((4 * tokens, width), BF),
            pltpu.VMEM((4 * tokens, width), F32),
        ],
        compiler_params=params(),
        cost_estimate=cost(),
    )(*norms, *streams, *ups, *downs)


def weight_grad_kernel(*refs):
    place, norms, streams, hidden, pre = refs[0], refs[1:5], refs[5:9], refs[9], refs[10]
    send, keep, norm_all, stream_all = refs[11:]
    tokens = norms[0].shape[0]
    chunk = pre.shape[1] // 4
    for t in range(4):
        norm_all[t * tokens : (t + 1) * tokens, :] = norms[t][...]
        stream_all[t * tokens : (t + 1) * tokens, :] = streams[t][...]
    for m in (1, 3, 0, 2):
        here = slice(m * chunk, (m + 1) * chunk)
        up = tn(norm_all[...], pre[:, here]).astype(BF)
        down = tn(hidden[:, here], stream_all[...]).astype(BF)
        target = send if m % 2 else keep
        side = lax.rem(place[4] + m // 2, 2)
        for n in range(8):
            block = slice(n * 128, (n + 1) * 128)
            target[n * 2 + side, :128, :] = up[block, :]
            target[n * 2 + side, 128:, :128] = down[:128, block]
            target[n * 2 + side, 128:, 128:] = down[128:, block]


def weight_grads(place, norms, streams, hidden, pre):
    tokens, width = norms[0].shape
    return pl.pallas_call(
        weight_grad_kernel,
        out_shape=[jax.ShapeDtypeStruct((16, 256, 256), BF)] * 2,
        in_specs=[SMEM] + [VMEM] * 10,
        out_specs=[VMEM] * 2,
        scratch_shapes=[pltpu.VMEM((4 * tokens, width), BF), pltpu.VMEM((4 * tokens, width), BF)],
        compiler_params=params(),
        cost_estimate=cost(),
    )(place, *norms, *streams, hidden, pre)


def add(a, b):
    return (a.astype(F32) + b.astype(F32)).astype(BF)


def pair_sum_kernel(keep, got, out):
    out[...] = add(keep[...], got[...])


def all_sum_kernel(blocks, merges, out, merge_out):
    total = blocks[0].astype(F32)
    merge = merges[0].astype(F32)
    for n in range(1, blocks.shape[0]):
        total += blocks[n].astype(F32)
        merge += merges[n].astype(F32)
    for n in range(4):
        merge_out[:, n * 256 : (n + 1) * 256] = merge[n * 16 : (n + 1) * 16, :]
    total = total.astype(BF)
    proj = merge[64:, :].astype(BF)
    for n in range(out.shape[0]):
        out[n, :256, :] = total
        out[n, 256:, :] = proj


def merge_pack_kernel(merge_keep, merge_got, proj_keep, proj_got, out):
    for p in range(out.shape[0]):
        merge = add(merge_keep[p], merge_got[p])
        for n in range(4):
            out[p, n * 16 : (n + 1) * 16, :] = merge[:, n * 256 : (n + 1) * 256]
        out[p, 64:, :] = add(proj_keep[p // 2], proj_got[p // 2])


def sums(kernel, shapes, *args):
    return pl.pallas_call(
        kernel,
        out_shape=[
            jax.ShapeDtypeStruct(shape, F32 if shape == (16, 1024) else BF) for shape in shapes
        ],
        in_specs=[VMEM] * len(args),
        out_specs=[VMEM] * len(shapes),
        compiler_params=params(),
        cost_estimate=cost(),
    )(*args)


def down_kernel(*refs):
    hidden, downs, parts = refs[0], refs[1:5], refs[5:]
    tokens = parts[0].shape[0]
    chunk = downs[0].shape[0]
    for t in range(4):
        rows = slice(t * tokens, (t + 1) * tokens)
        total = 0.0
        for m in range(4):
            total += jnp.dot(
                hidden[rows, m * chunk : (m + 1) * chunk],
                downs[m][...],
                preferred_element_type=F32,
            )
        parts[t][...] = total.astype(BF)


def down_parts(hidden, downs):
    tokens = hidden.shape[0] // 4
    return pl.pallas_call(
        down_kernel,
        out_shape=[jax.ShapeDtypeStruct((tokens, downs[0].shape[1]), BF)] * 4,
        in_specs=[VMEM] * 5,
        out_specs=[VMEM] * 4,
        compiler_params=params(),
        cost_estimate=cost(),
    )(hidden, *downs)


def merge_grad_kernel(place, left, right0, right1, right2, right3, keep, send, both, left_all, right_all):
    tokens, width = left.shape[1:]
    for t, right in enumerate((right0, right1, right2, right3)):
        left_all[t * tokens : (t + 1) * tokens, :] = left[lax.rem(place[2] + 4 - t, 4)]
        right_all[t * tokens : (t + 1) * tokens, :] = right[...]
    part = tn(left_all[...], right_all[...]).astype(BF)
    for n in range(width // 16):
        both[lax.rem(n % 2 + place[5], 2), n // 2] = part[n * 16 : (n + 1) * 16, :]
    keep[...] = both[0]
    send[...] = both[1]


def merge_grads(place, left, rights):
    tokens, width = left.shape[1:]
    last = rights[0].shape[-1]
    return pl.pallas_call(
        merge_grad_kernel,
        out_shape=[jax.ShapeDtypeStruct((width // 32, 16, last), BF)] * 2,
        in_specs=[SMEM] + [VMEM] * 5,
        out_specs=[VMEM] * 2,
        scratch_shapes=[
            pltpu.VMEM((2, width // 32, 16, last), BF),
            pltpu.VMEM((4 * tokens, width), BF),
            pltpu.VMEM((4 * tokens, last), BF),
        ],
        compiler_params=params(),
        cost_estimate=cost(),
    )(place, left, *rights)


def place_kernel(blocks, up, down):
    for n in range(8):
        block = slice(n * 128, (n + 1) * 128)
        up[block, :] = blocks[n, :128, :].astype(F32)
        down[:128, block] = blocks[n, 128:256, :128].astype(F32)
        down[128:, block] = blocks[n, 128:256, 128:].astype(F32)


def place_blocks(blocks):
    return pl.pallas_call(
        place_kernel,
        out_shape=[
            jax.ShapeDtypeStruct((1024, 256), F32),
            jax.ShapeDtypeStruct((256, 1024), F32),
        ],
        in_specs=[VMEM],
        out_specs=[VMEM] * 2,
        compiler_params=params(),
        cost_estimate=cost(),
    )(blocks)


def proj_kernel(place, own, other, out):
    for k in range(4):
        y = lax.rem(place[2] + 4 - k, 4)
        for side, ref in enumerate((own, other)):
            c = lax.rem(place[5] + side, 2)
            for n in range(8):
                start = pl.multiple_of((y * 16 + c * 8 + n) * 8, 8)
                block = ref[k, n].astype(F32)
                out[pl.ds(start, 8), :256] = block[:8, :]
                out[pl.ds(start, 8), 256:] = block[8:, :]


def place_proj(place, own, other):
    return pl.pallas_call(
        proj_kernel,
        out_shape=jax.ShapeDtypeStruct((512, 512), F32),
        in_specs=[SMEM] + [VMEM] * 2,
        out_specs=VMEM,
        compiler_params=params(),
        cost_estimate=cost(),
    )(place, own, other)


def norm_back(values, gain, upstream):
    center = values - jnp.mean(values, axis=-1, keepdims=True)
    spread = jnp.mean(center * center, axis=-1, keepdims=True)
    factor = lax.rsqrt(spread + 1e-05)
    normal = center * factor
    scaled = upstream * gain
    return factor * (
        scaled
        - jnp.mean(scaled, axis=-1, keepdims=True)
        - normal * jnp.mean(scaled * normal, axis=-1, keepdims=True)
    )


def skip_kernel(
    place, coarse_grad, gain, merge, merged, att, skip, proj0, proj1, proj2, proj3, hold, blocks
):
    lanes = hold.shape[0]
    width = lanes * 128
    half_rows, half_cols = hold.shape[1] // 2, hold.shape[2] // 2
    grad = nt(coarse_grad[...], merge[...])
    grad = norm_back(merged[...].astype(F32), gain[...], grad).astype(BF)
    total = None
    for p in range(4):
        di, dj = p % 2, p // 2
        piece = grad[:, p * width : (p + 1) * width]
        part = tn(att[:, p * width : (p + 1) * width], piece)
        total = part if total is None else total + part
        wide = piece.astype(F32)
        for n in range(lanes):
            for i in range(half_rows):
                hold[n, di + 2 * i, pl.ds(dj, half_cols, stride=2), :] = wide[
                    i * half_cols : (i + 1) * half_cols, n * 128 : (n + 1) * 128
                ]
    for n in range(lanes):
        skip[:, :, n * 128 : (n + 1) * 128] = hold[n].astype(BF)
    for n in range(width // 8):
        dy = lax.rem(n // 16 + 4 - place[2], 4)
        dc = lax.rem(n // 8 % 2 + place[5], 2)
        rows = slice(n * 8, (n + 1) * 8)
        block = jnp.concatenate([total[rows, : width // 2], total[rows, width // 2 :]], axis=0)
        blocks[dy, dc, n % 8] = block.astype(BF)
    for n, out in enumerate((proj0, proj1, proj2, proj3)):
        out[...] = blocks[n]


def skip_grads(place, coarse_grad, gain, merge, merged, att, rows, cols):
    width = att.shape[1] // 4
    return pl.pallas_call(
        skip_kernel,
        out_shape=[
            jax.ShapeDtypeStruct((rows, cols, width), BF),
        ]
        + [jax.ShapeDtypeStruct((2, 8, 16, width // 2), BF)] * 4,
        in_specs=[SMEM] + [VMEM] * 5,
        out_specs=[VMEM] * 5,
        scratch_shapes=[
            pltpu.VMEM((width // 128, rows, cols, 128), F32),
            pltpu.VMEM((4, 2, 8, 16, width // 2), BF),
        ],
        compiler_params=params(),
        cost_estimate=cost(),
    )(place, coarse_grad, gain.reshape(1, -1), merge, merged, att)


def per_device(
    level_one, gain_attn, w_qkv, w_proj, gain_merge, w_merge, gain_mlp, w_up, w_down, cotangent
):
    tile_rows, tile_cols, feature = level_one.shape
    width = cotangent.shape[-1]
    upstream = cotangent.reshape(-1, width)
    place = jnp.stack(
        [lax.axis_index(LAT), jnp.int32(lax.axis_size(LAT))]
        + [lax.axis_index(name) for name in ("y", "z", "xl", "c", "xh")]
    ).astype(jnp.int32)

    top = rotate(level_one[-SHIFT:], LAT, 1)
    bottom = rotate(level_one[:SHIFT], LAT, -1)
    top, bottom = together(top, bottom)

    tall = [top, level_one, bottom]
    left = rotate(jnp.concatenate([part[:, -SHIFT:] for part in tall], axis=0), LON, 1)
    right = rotate(jnp.concatenate([part[:, :SHIFT] for part in tall], axis=0), LON, -1)
    left, right, first_up, first_down, upstream = together(
        left, right, w_up, w_down, upstream
    )

    coarse_norm, coarse, merged, picks, att = attend(
        place, level_one, top, bottom, left, right, gain_attn, w_qkv, w_proj,
        gain_merge, w_merge, gain_mlp,
    )
    up_x, up_c = rotate(first_up, "xl", 1), rotate(first_up, "c", 1)
    streams = gather_rel(upstream, "y")
    coarse_norm, picks, up_x, up_c, streams, first_down = together(
        coarse_norm, picks, up_x, up_c, streams, first_down
    )

    down_x, up_xc = rotate(first_down, "xl", 1), rotate(up_x, "c", 1)
    norms = gather_rel(coarse_norm, "y")
    norms, up_xc, down_x, picks, first_down = together(norms, up_xc, down_x, picks, first_down)

    down_c, down_xc = rotate(first_down, "c", 1), rotate(down_x, "c", 1)
    lefts = lax.all_to_all(picks, "y", 0, 0)
    ups, downs = [w_up, up_c, up_x, up_xc], [w_down, down_c, down_x, down_xc]
    *parts, hidden, grad_pre = hidden_units(norms, streams, ups, downs)
    parts, hidden, grad_pre, lefts = together(parts, hidden, grad_pre, lefts)

    arrived = [rotate(parts[k], "y", -k) for k in range(1, 4)]
    send, keep = weight_grads(place, norms, streams, hidden, grad_pre)
    (blocks,) = sums(pair_sum_kernel, [(16, 256, 256)], keep, rotate(send, "c", 1))
    arrived, blocks = together(arrived, blocks)
    grad_norm = sum(part.astype(F32) for part in [parts[0]] + arrived)
    grad_coarse = (
        upstream.astype(F32) + norm_back(coarse.astype(F32), gain_mlp, grad_norm)
    ).astype(BF)

    blocks = lax.all_to_all(blocks, LAT + ("xl",), 0, 0)
    rights = gather_rel(grad_coarse, "y")
    grad_skip, *projs = skip_grads(
        place, grad_coarse, gain_merge, w_merge, merged, att, tile_rows, tile_cols
    )
    rights, projs, hidden = together(rights, projs, hidden)
    proj = sum(
        part.astype(F32)
        for part in [projs[0]] + [rotate(projs[k], "y", k) for k in range(1, 4)]
    ).astype(BF)
    proj_got = rotate(proj[1], "c", 1)
    merge_keep, merge_send = merge_grads(place, lefts, rights)
    merge_got = rotate(merge_send, "c", 1)
    (merges,) = sums(
        merge_pack_kernel, [(16, 80, 256)], merge_keep, merge_got, proj[0], proj_got
    )
    blocks, merges, hidden = together(blocks, merges, hidden)

    merges = lax.all_to_all(merges, LAT + ("xl",), 0, 0)
    outer = down_parts(hidden, downs)
    merges, outer = together(merges, outer)

    blocks, grad_merge = sums(all_sum_kernel, [(8, 272, 256), (16, 1024)], blocks, merges)
    blocks = lax.all_to_all(blocks, LAT, 0, 0)
    summed = scatter_rel(outer, "y", -1)
    level_two = (coarse.astype(F32) + summed).astype(BF)
    blocks, level_two = together(blocks, level_two)

    proj = jnp.stack(gather_rel(blocks[:, 256:], "y"))
    grad_up, grad_down = place_blocks(blocks)
    grad_proj = place_proj(place, proj, rotate(proj, "c", 1))

    level_two = level_two.reshape(tile_rows // 2, tile_cols // 2, width)
    return (level_two, grad_skip, grad_proj, grad_merge, grad_up, grad_down)


def solution(mesh):
    fine = Mesh(mesh.devices.reshape(2, 4, 4, 2, 2), LAT + LON)
    grid = P(LAT, LON, None)
    placed = (grid, P(), P(), P(), P(), P(), P(), P(None, LON), P(LON, None), grid)
    return jax.shard_map(
        per_device,
        mesh=fine,
        in_specs=placed,
        out_specs=(grid, grid, P(), P(LAT + LON, None), P(None, LON), P(LON, None)),
        check_vma=False,
    )
```

```python
import jax
import jax.numpy as jnp
from jax import lax
from jax.experimental import pallas as pl
from jax.experimental.pallas import tpu as pltpu
from jax.sharding import Mesh
from jax.sharding import PartitionSpec as P

HD = 64
WIN = 8
SHIFT = 4
LAT = ("xh", "z")
LON = ("y", "xl", "c")
F32 = jnp.float32
BF = jnp.bfloat16
VMEM = pl.BlockSpec(memory_space=pltpu.VMEM)
HBM = pl.BlockSpec(memory_space=pl.ANY)
SMEM = pl.BlockSpec(memory_space=pltpu.SMEM)


def rotate(value, axis, shift):
    size = lax.axis_size(axis)
    return lax.ppermute(value, axis, [(i, (i + shift) % size) for i in range(size)])


def params():
    return pltpu.CompilerParams(vmem_limit_bytes=62 * 2**20)


def cost():
    return pl.CostEstimate(flops=1000, bytes_accessed=1000, transcendentals=0)


def together(*values):
    return lax.optimization_barrier(values)


def scatter_rel(parts, axis, way):
    total = parts[0].astype(F32)
    for k in range(1, len(parts)):
        total = total + rotate(parts[k], axis, way * k).astype(F32)
    return total


def gather_rel(value, axis):
    return [value] + [rotate(value, axis, k) for k in range(1, lax.axis_size(axis))]


def normalise(values, gain):
    center = values - jnp.mean(values, axis=-1, keepdims=True)
    spread = jnp.mean(center * center, axis=-1, keepdims=True)
    return center * lax.rsqrt(spread + 1e-05) * gain


def nt(a, b):
    return lax.dot_general(a, b, (((1,), (1,)), ((), ())), preferred_element_type=F32)


def tn(a, b):
    return lax.dot_general(a, b, (((0,), (0,)), ((), ())), preferred_element_type=F32)


def attend_kernel(
    place_ref, own_ref, top_ref, bottom_ref, left_ref, right_ref, gain_attn_ref, qkv_ref, proj_ref,
    gain_merge_ref, merge_ref, gain_mlp_ref,
    norm_out, coarse_out, merged_out, pick_out, att_out,
    field, att, hold, proj_all, merge_all, proj_sem, merge_sem,
):
    proj_copy = pltpu.make_async_copy(proj_ref, proj_all, proj_sem)
    merge_copy = pltpu.make_async_copy(merge_ref, merge_all, merge_sem)
    proj_copy.start()
    merge_copy.start()
    rows, cols, width = own_ref.shape
    lanes = width // 128
    for n in range(lanes):
        part = slice(n * 128, (n + 1) * 128)
        field[n, SHIFT : SHIFT + rows, SHIFT : SHIFT + cols, :] = own_ref[:, :, part].astype(F32)
        field[n, :SHIFT, SHIFT : SHIFT + cols, :] = top_ref[:, :, part].astype(F32)
        field[n, SHIFT + rows :, SHIFT : SHIFT + cols, :] = bottom_ref[:, :, part].astype(F32)
        field[n, :, :SHIFT, :] = left_ref[:, :, part].astype(F32)
        field[n, :, SHIFT + cols :, :] = right_ref[:, :, part].astype(F32)
    across = (cols + WIN) // WIN
    size = WIN * WIN
    low = lax.broadcasted_iota(jnp.int32, (size, 128), 1) < HD
    key_row = lax.broadcasted_iota(jnp.int32, (2 * size, size), 1) // WIN
    first = place_ref[0] * rows - SHIFT
    total = place_ref[1] * rows

    def band(a, carry):
        for b in range(across):
            x = jnp.concatenate(
                [
                    field[n, pl.ds(a * WIN, WIN), b * WIN : (b + 1) * WIN, :].reshape(size, 128)
                    for n in range(lanes)
                ],
                axis=1,
            )
            hold[b * size : (b + 1) * size, :] = normalise(x, gain_attn_ref[...]).astype(BF)
        qkv = jnp.dot(hold[...], qkv_ref[...], preferred_element_type=F32).astype(BF)
        row = first + a * WIN + key_row
        allowed = (row >= 0) & (row < total)
        for b in range(across):
            here = slice(b * size, (b + 1) * size)
            for p in range(lanes):
                q = qkv[here, p * 128 : (p + 1) * 128]
                k = qkv[here, width + p * 128 : width + (p + 1) * 128]
                v = qkv[here, 2 * width + p * 128 : 2 * width + (p + 1) * 128]
                none = jnp.zeros_like(q)
                pair = jnp.concatenate([jnp.where(low, q, none), jnp.where(low, none, q)], axis=0)
                scores = jnp.where(allowed, nt(pair, k) * (1.0 / 8.0), -1e30)
                expo = jnp.exp(scores - jnp.max(scores, axis=1, keepdims=True))
                weights = (expo / jnp.sum(expo, axis=1, keepdims=True)).astype(BF)
                both = jnp.dot(weights, v, preferred_element_type=F32)
                out = jnp.where(low, both[:size], both[size:]).astype(BF).astype(F32)
                att[p, pl.ds(a * WIN, WIN), b * WIN : (b + 1) * WIN, :] = out.reshape(WIN, WIN, 128)
        return carry

    lax.fori_loop(0, (rows + WIN) // WIN, band, 0)

    proj_copy.wait()
    half_rows, half_cols = rows // 2, cols // 2
    tokens = half_rows * half_cols
    pieces = []
    for p in range(4):
        di, dj = p % 2, p // 2
        def pick(ref):
            return jnp.concatenate(
                [
                    jnp.concatenate(
                        [
                            ref[n, SHIFT + di + 2 * i, pl.ds(SHIFT + dj, half_cols, stride=2), :]
                            for i in range(half_rows)
                        ],
                        axis=0,
                    )
                    for n in range(lanes)
                ],
                axis=1,
            )
        got = pick(att).astype(BF)
        att_out[:, p * width : (p + 1) * width] = got
        block = pick(field) + jnp.dot(got, proj_all[...], preferred_element_type=F32)
        block = block.astype(BF)
        merged_out[:, p * width : (p + 1) * width] = block
    merged = merged_out[...].astype(F32)
    merged_norm = normalise(merged, gain_merge_ref[...]).astype(BF)
    for n in range(4):
        pick_out[n] = jnp.concatenate(
            [merged_norm[:, g * 256 + n * 64 : g * 256 + (n + 1) * 64] for g in range(8)], axis=1
        )
    merge_copy.wait()
    coarse = jnp.dot(merged_norm, merge_all[...], preferred_element_type=F32).astype(BF)
    coarse_out[...] = coarse
    norm_out[...] = normalise(coarse.astype(F32), gain_mlp_ref[...]).astype(BF)


def attend(place, own, top, bottom, left, right, gain_attn, w_qkv, w_proj, gain_merge, w_merge, gain_mlp):
    rows, cols, width = own.shape
    tokens = rows * cols // 4
    wide = w_merge.shape[1]
    shapes = [
        jax.ShapeDtypeStruct((tokens, wide), BF),
        jax.ShapeDtypeStruct((tokens, wide), BF),
        jax.ShapeDtypeStruct((tokens, 4 * width), BF),
        jax.ShapeDtypeStruct((4, tokens, width), BF),
        jax.ShapeDtypeStruct((tokens, 4 * width), BF),
    ]
    return pl.pallas_call(
        attend_kernel,
        out_shape=shapes,
        in_specs=[SMEM]
        + [VMEM] * 7
        + [HBM, VMEM, HBM, VMEM],
        out_specs=[VMEM] * 5,
        scratch_shapes=[
            pltpu.VMEM((width // 128, rows + WIN, cols + WIN, 128), F32),
            pltpu.VMEM((width // 128, rows + WIN, cols + WIN, 128), F32),
            pltpu.VMEM(((cols + WIN) * WIN, width), BF),
            pltpu.VMEM(w_proj.shape, BF),
            pltpu.VMEM(w_merge.shape, BF),
            pltpu.SemaphoreType.DMA,
            pltpu.SemaphoreType.DMA,
        ],
        compiler_params=params(),
        cost_estimate=cost(),
    )(place, own, top, bottom, left, right, gain_attn.reshape(1, -1), w_qkv, w_proj, gain_merge.reshape(1, -1), w_merge, gain_mlp.reshape(1, -1))


def hidden_kernel(*refs):
    norms, streams, ups, downs, parts = (refs[i : i + 4] for i in range(0, 20, 4))
    hidden_out, pre_out, norm_all, stream_all, total = refs[20:]
    tokens = norms[0].shape[0]
    chunk = ups[0].shape[1]
    for t in range(4):
        norm_all[t * tokens : (t + 1) * tokens, :] = norms[t][...]
        stream_all[t * tokens : (t + 1) * tokens, :] = streams[t][...]
    for m in range(4):
        up = ups[m][...]
        pre = jnp.dot(norm_all[...], up, preferred_element_type=F32)
        grad_hidden = nt(stream_all[...], downs[m][...])
        tangent = jnp.tanh(0.7978845608 * (pre + 0.044715 * pre * pre * pre))
        hidden = 0.5 * pre * (1.0 + tangent)
        slope = 0.5 * (1.0 + tangent) + 0.5 * pre * (1.0 - tangent * tangent) * 0.7978845608 * (
            1.0 + 3.0 * 0.044715 * pre * pre
        )
        here = slice(m * chunk, (m + 1) * chunk)
        hidden_out[:, here] = hidden.astype(BF)
        grad_pre = (grad_hidden * slope).astype(BF)
        pre_out[:, here] = grad_pre
        part = nt(grad_pre, up)
        if m == 0:
            total[...] = part
        elif m < 3:
            total[...] += part
        else:
            for t in range(4):
                rows = slice(t * tokens, (t + 1) * tokens)
                parts[t][...] = (total[rows, :] + part[rows, :]).astype(BF)


def hidden_units(norms, streams, ups, downs):
    tokens, width = norms[0].shape
    chunk = ups[0].shape[1]
    out = [jax.ShapeDtypeStruct((tokens, width), BF)] * 4
    out += [jax.ShapeDtypeStruct((4 * tokens, 4 * chunk), BF)] * 2
    return pl.pallas_call(
        hidden_kernel,
        out_shape=out,
        in_specs=[VMEM] * 16,
        out_specs=[VMEM] * 6,
        scratch_shapes=[
            pltpu.VMEM((4 * tokens, width), BF),
            pltpu.VMEM((4 * tokens, width), BF),
            pltpu.VMEM((4 * tokens, width), F32),
        ],
        compiler_params=params(),
        cost_estimate=cost(),
    )(*norms, *streams, *ups, *downs)


def weight_grad_kernel(*refs):
    place, norms, streams, hidden, pre = refs[0], refs[1:5], refs[5:9], refs[9], refs[10]
    send, keep, norm_all, stream_all = refs[11:]
    tokens = norms[0].shape[0]
    chunk = pre.shape[1] // 4
    for t in range(4):
        norm_all[t * tokens : (t + 1) * tokens, :] = norms[t][...]
        stream_all[t * tokens : (t + 1) * tokens, :] = streams[t][...]
    for m in (1, 3, 0, 2):
        here = slice(m * chunk, (m + 1) * chunk)
        up = tn(norm_all[...], pre[:, here]).astype(BF)
        down = tn(hidden[:, here], stream_all[...]).astype(BF)
        target = send if m % 2 else keep
        side = lax.rem(place[4] + m // 2, 2)
        for n in range(8):
            block = slice(n * 128, (n + 1) * 128)
            target[n * 2 + side, :128, :] = up[block, :]
            target[n * 2 + side, 128:, :128] = down[:128, block]
            target[n * 2 + side, 128:, 128:] = down[128:, block]


def weight_grads(place, norms, streams, hidden, pre):
    tokens, width = norms[0].shape
    return pl.pallas_call(
        weight_grad_kernel,
        out_shape=[jax.ShapeDtypeStruct((16, 256, 256), BF)] * 2,
        in_specs=[SMEM] + [VMEM] * 10,
        out_specs=[VMEM] * 2,
        scratch_shapes=[pltpu.VMEM((4 * tokens, width), BF), pltpu.VMEM((4 * tokens, width), BF)],
        compiler_params=params(),
        cost_estimate=cost(),
    )(place, *norms, *streams, hidden, pre)


def add(a, b):
    return (a.astype(F32) + b.astype(F32)).astype(BF)


def pair_sum_kernel(keep, got, out):
    out[...] = add(keep[...], got[...])


def all_sum_kernel(blocks, merges, out, merge_out):
    total = blocks[0].astype(F32)
    merge = merges[0].astype(F32)
    for n in range(1, blocks.shape[0]):
        total += blocks[n].astype(F32)
        merge += merges[n].astype(F32)
    for n in range(4):
        merge_out[:, n * 256 : (n + 1) * 256] = merge[n * 16 : (n + 1) * 16, :]
    total = total.astype(BF)
    proj = merge[64:, :].astype(BF)
    for n in range(out.shape[0]):
        out[n, :256, :] = total
        out[n, 256:, :] = proj


def merge_pack_kernel(merge_keep, merge_got, proj_keep, proj_got, out):
    for p in range(out.shape[0]):
        merge = add(merge_keep[p], merge_got[p])
        for n in range(4):
            out[p, n * 16 : (n + 1) * 16, :] = merge[:, n * 256 : (n + 1) * 256]
        out[p, 64:, :] = add(proj_keep[p // 2], proj_got[p // 2])


def sums(kernel, shapes, *args):
    return pl.pallas_call(
        kernel,
        out_shape=[
            jax.ShapeDtypeStruct(shape, F32 if shape == (16, 1024) else BF) for shape in shapes
        ],
        in_specs=[VMEM] * len(args),
        out_specs=[VMEM] * len(shapes),
        compiler_params=params(),
        cost_estimate=cost(),
    )(*args)


def down_kernel(*refs):
    hidden, downs, parts = refs[0], refs[1:5], refs[5:]
    tokens = parts[0].shape[0]
    chunk = downs[0].shape[0]
    for t in range(4):
        rows = slice(t * tokens, (t + 1) * tokens)
        total = 0.0
        for m in range(4):
            total += jnp.dot(
                hidden[rows, m * chunk : (m + 1) * chunk],
                downs[m][...],
                preferred_element_type=F32,
            )
        parts[t][...] = total.astype(BF)


def down_parts(hidden, downs):
    tokens = hidden.shape[0] // 4
    return pl.pallas_call(
        down_kernel,
        out_shape=[jax.ShapeDtypeStruct((tokens, downs[0].shape[1]), BF)] * 4,
        in_specs=[VMEM] * 5,
        out_specs=[VMEM] * 4,
        compiler_params=params(),
        cost_estimate=cost(),
    )(hidden, *downs)


def merge_grad_kernel(place, left, right0, right1, right2, right3, keep, send, both, left_all, right_all):
    tokens, width = left.shape[1:]
    for t, right in enumerate((right0, right1, right2, right3)):
        left_all[t * tokens : (t + 1) * tokens, :] = left[lax.rem(place[2] + 4 - t, 4)]
        right_all[t * tokens : (t + 1) * tokens, :] = right[...]
    part = tn(left_all[...], right_all[...]).astype(BF)
    for n in range(width // 16):
        both[lax.rem(n % 2 + place[5], 2), n // 2] = part[n * 16 : (n + 1) * 16, :]
    keep[...] = both[0]
    send[...] = both[1]


def merge_grads(place, left, rights):
    tokens, width = left.shape[1:]
    last = rights[0].shape[-1]
    return pl.pallas_call(
        merge_grad_kernel,
        out_shape=[jax.ShapeDtypeStruct((width // 32, 16, last), BF)] * 2,
        in_specs=[SMEM] + [VMEM] * 5,
        out_specs=[VMEM] * 2,
        scratch_shapes=[
            pltpu.VMEM((2, width // 32, 16, last), BF),
            pltpu.VMEM((4 * tokens, width), BF),
            pltpu.VMEM((4 * tokens, last), BF),
        ],
        compiler_params=params(),
        cost_estimate=cost(),
    )(place, left, *rights)


def place_kernel(blocks, up, down):
    for n in range(8):
        block = slice(n * 128, (n + 1) * 128)
        up[block, :] = blocks[n, :128, :].astype(F32)
        down[:128, block] = blocks[n, 128:256, :128].astype(F32)
        down[128:, block] = blocks[n, 128:256, 128:].astype(F32)


def place_blocks(blocks):
    return pl.pallas_call(
        place_kernel,
        out_shape=[
            jax.ShapeDtypeStruct((1024, 256), F32),
            jax.ShapeDtypeStruct((256, 1024), F32),
        ],
        in_specs=[VMEM],
        out_specs=[VMEM] * 2,
        compiler_params=params(),
        cost_estimate=cost(),
    )(blocks)


def proj_kernel(place, own, other, out):
    for k in range(4):
        y = lax.rem(place[2] + 4 - k, 4)
        for side, ref in enumerate((own, other)):
            c = lax.rem(place[5] + side, 2)
            for n in range(8):
                start = pl.multiple_of((y * 16 + c * 8 + n) * 8, 8)
                block = ref[k, n].astype(F32)
                out[pl.ds(start, 8), :256] = block[:8, :]
                out[pl.ds(start, 8), 256:] = block[8:, :]


def place_proj(place, own, other):
    return pl.pallas_call(
        proj_kernel,
        out_shape=jax.ShapeDtypeStruct((512, 512), F32),
        in_specs=[SMEM] + [VMEM] * 2,
        out_specs=VMEM,
        compiler_params=params(),
        cost_estimate=cost(),
    )(place, own, other)


def norm_back(values, gain, upstream):
    center = values - jnp.mean(values, axis=-1, keepdims=True)
    spread = jnp.mean(center * center, axis=-1, keepdims=True)
    factor = lax.rsqrt(spread + 1e-05)
    normal = center * factor
    scaled = upstream * gain
    return factor * (
        scaled
        - jnp.mean(scaled, axis=-1, keepdims=True)
        - normal * jnp.mean(scaled * normal, axis=-1, keepdims=True)
    )


def skip_kernel(
    place, coarse_grad, gain, merge, merged, att, skip, proj0, proj1, proj2, proj3, hold, blocks
):
    lanes = hold.shape[0]
    width = lanes * 128
    half_rows, half_cols = hold.shape[1] // 2, hold.shape[2] // 2
    grad = nt(coarse_grad[...], merge[...])
    grad = norm_back(merged[...].astype(F32), gain[...], grad).astype(BF)
    total = None
    for p in range(4):
        di, dj = p % 2, p // 2
        piece = grad[:, p * width : (p + 1) * width]
        part = tn(att[:, p * width : (p + 1) * width], piece)
        total = part if total is None else total + part
        wide = piece.astype(F32)
        for n in range(lanes):
            for i in range(half_rows):
                hold[n, di + 2 * i, pl.ds(dj, half_cols, stride=2), :] = wide[
                    i * half_cols : (i + 1) * half_cols, n * 128 : (n + 1) * 128
                ]
    for n in range(lanes):
        skip[:, :, n * 128 : (n + 1) * 128] = hold[n].astype(BF)
    for n in range(width // 8):
        dy = lax.rem(n // 16 + 4 - place[2], 4)
        dc = lax.rem(n // 8 % 2 + place[5], 2)
        rows = slice(n * 8, (n + 1) * 8)
        block = jnp.concatenate([total[rows, : width // 2], total[rows, width // 2 :]], axis=0)
        blocks[dy, dc, n % 8] = block.astype(BF)
    for n, out in enumerate((proj0, proj1, proj2, proj3)):
        out[...] = blocks[n]


def skip_grads(place, coarse_grad, gain, merge, merged, att, rows, cols):
    width = att.shape[1] // 4
    return pl.pallas_call(
        skip_kernel,
        out_shape=[
            jax.ShapeDtypeStruct((rows, cols, width), BF),
        ]
        + [jax.ShapeDtypeStruct((2, 8, 16, width // 2), BF)] * 4,
        in_specs=[SMEM] + [VMEM] * 5,
        out_specs=[VMEM] * 5,
        scratch_shapes=[
            pltpu.VMEM((width // 128, rows, cols, 128), F32),
            pltpu.VMEM((4, 2, 8, 16, width // 2), BF),
        ],
        compiler_params=params(),
        cost_estimate=cost(),
    )(place, coarse_grad, gain.reshape(1, -1), merge, merged, att)


def per_device(
    level_one, gain_attn, w_qkv, w_proj, gain_merge, w_merge, gain_mlp, w_up, w_down, cotangent
):
    tile_rows, tile_cols, feature = level_one.shape
    width = cotangent.shape[-1]
    upstream = cotangent.reshape(-1, width)
    place = jnp.stack(
        [lax.axis_index(LAT), jnp.int32(lax.axis_size(LAT))]
        + [lax.axis_index(name) for name in ("y", "z", "xl", "c", "xh")]
    ).astype(jnp.int32)

    top = rotate(level_one[-SHIFT:], LAT, 1)
    bottom = rotate(level_one[:SHIFT], LAT, -1)
    top, bottom = together(top, bottom)

    tall = [top, level_one, bottom]
    left = rotate(jnp.concatenate([part[:, -SHIFT:] for part in tall], axis=0), LON, 1)
    right = rotate(jnp.concatenate([part[:, :SHIFT] for part in tall], axis=0), LON, -1)
    left, right, first_up, first_down, upstream = together(
        left, right, w_up, w_down, upstream
    )

    coarse_norm, coarse, merged, picks, att = attend(
        place, level_one, top, bottom, left, right, gain_attn, w_qkv, w_proj,
        gain_merge, w_merge, gain_mlp,
    )
    up_x, up_c = rotate(first_up, "xl", 1), rotate(first_up, "c", 1)
    streams = gather_rel(upstream, "y")
    coarse_norm, picks, up_x, up_c, streams, first_down = together(
        coarse_norm, picks, up_x, up_c, streams, first_down
    )

    down_x, up_xc = rotate(first_down, "xl", 1), rotate(up_x, "c", 1)
    norms = gather_rel(coarse_norm, "y")
    norms, up_xc, down_x, picks, first_down = together(norms, up_xc, down_x, picks, first_down)

    down_c, down_xc = rotate(first_down, "c", 1), rotate(down_x, "c", 1)
    lefts = lax.all_to_all(picks, "y", 0, 0)
    ups, downs = [w_up, up_c, up_x, up_xc], [w_down, down_c, down_x, down_xc]
    *parts, hidden, grad_pre = hidden_units(norms, streams, ups, downs)
    parts, hidden, grad_pre, lefts = together(parts, hidden, grad_pre, lefts)

    arrived = [rotate(parts[k], "y", -k) for k in range(1, 4)]
    send, keep = weight_grads(place, norms, streams, hidden, grad_pre)
    (blocks,) = sums(pair_sum_kernel, [(16, 256, 256)], keep, rotate(send, "c", 1))
    outer = down_parts(hidden, downs)
    arrived, outer = together(arrived, outer)
    grad_norm = sum(part.astype(F32) for part in [parts[0]] + arrived)
    grad_coarse = (
        upstream.astype(F32) + norm_back(coarse.astype(F32), gain_mlp, grad_norm)
    ).astype(BF)

    blocks = lax.all_to_all(blocks, LAT + ("xl",), 0, 0)
    rights = gather_rel(grad_coarse, "y")
    grad_skip, *projs = skip_grads(
        place, grad_coarse, gain_merge, w_merge, merged, att, tile_rows, tile_cols
    )
    rights, grad_skip = together(rights, grad_skip)
    proj = sum(
        part.astype(F32)
        for part in [projs[0]] + [rotate(projs[k], "y", k) for k in range(1, 4)]
    ).astype(BF)
    proj_got = rotate(proj[1], "c", 1)
    merge_keep, merge_send = merge_grads(place, lefts, rights)
    merge_got = rotate(merge_send, "c", 1)
    (merges,) = sums(
        merge_pack_kernel, [(16, 80, 256)], merge_keep, merge_got, proj[0], proj_got
    )
    blocks, merges, outer = together(blocks, merges, outer)

    merges = lax.all_to_all(merges, LAT + ("xl",), 0, 0)
    merges, outer = together(merges, outer)

    blocks, grad_merge = sums(all_sum_kernel, [(8, 272, 256), (16, 1024)], blocks, merges)
    blocks = lax.all_to_all(blocks, LAT, 0, 0)
    summed = scatter_rel(outer, "y", -1)
    level_two = (coarse.astype(F32) + summed).astype(BF)
    blocks, level_two = together(blocks, level_two)

    proj = jnp.stack(gather_rel(blocks[:, 256:], "y"))
    grad_up, grad_down = place_blocks(blocks)
    grad_proj = place_proj(place, proj, rotate(proj, "c", 1))

    level_two = level_two.reshape(tile_rows // 2, tile_cols // 2, width)
    return (level_two, grad_skip, grad_proj, grad_merge, grad_up, grad_down)


def solution(mesh):
    fine = Mesh(mesh.devices.reshape(2, 4, 4, 2, 2), LAT + LON)
    grid = P(LAT, LON, None)
    placed = (grid, P(), P(), P(), P(), P(), P(), P(None, LON), P(LON, None), grid)
    return jax.shard_map(
        per_device,
        mesh=fine,
        in_specs=placed,
        out_specs=(grid, grid, P(), P(LAT + LON, None), P(None, LON), P(LON, None)),
        check_vma=False,
    )
```

```python
import jax
import jax.numpy as jnp
from jax import lax
from jax.experimental import pallas as pl
from jax.experimental.pallas import tpu as pltpu
from jax.sharding import Mesh
from jax.sharding import PartitionSpec as P

HD = 64
WIN = 8
SHIFT = 4
LAT = ("xh", "z")
LON = ("y", "xl", "c")
F32 = jnp.float32
BF = jnp.bfloat16
VMEM = pl.BlockSpec(memory_space=pltpu.VMEM)
HBM = pl.BlockSpec(memory_space=pl.ANY)
SMEM = pl.BlockSpec(memory_space=pltpu.SMEM)


def rotate(value, axis, shift):
    size = lax.axis_size(axis)
    return lax.ppermute(value, axis, [(i, (i + shift) % size) for i in range(size)])


def params():
    return pltpu.CompilerParams(vmem_limit_bytes=62 * 2**20)


def cost():
    return pl.CostEstimate(flops=1000, bytes_accessed=1000, transcendentals=0)


def together(*values):
    return lax.optimization_barrier(values)


def scatter_rel(parts, axis, way):
    total = parts[0].astype(F32)
    for k in range(1, len(parts)):
        total = total + rotate(parts[k], axis, way * k).astype(F32)
    return total


def gather_rel(value, axis):
    return [value] + [rotate(value, axis, k) for k in range(1, lax.axis_size(axis))]


def normalise(values, gain):
    center = values - jnp.mean(values, axis=-1, keepdims=True)
    spread = jnp.mean(center * center, axis=-1, keepdims=True)
    return center * lax.rsqrt(spread + 1e-05) * gain


def nt(a, b):
    return lax.dot_general(a, b, (((1,), (1,)), ((), ())), preferred_element_type=F32)


def tn(a, b):
    return lax.dot_general(a, b, (((0,), (0,)), ((), ())), preferred_element_type=F32)


def attend_kernel(
    place_ref, own_ref, top_ref, bottom_ref, left_ref, right_ref, gain_attn_ref, qkv_ref, proj_ref,
    gain_merge_ref, merge_ref, gain_mlp_ref,
    norm_out, coarse_out, merged_out, pick_out, att_out,
    field, att, hold, proj_all, merge_all, proj_sem, merge_sem,
):
    proj_copy = pltpu.make_async_copy(proj_ref, proj_all, proj_sem)
    merge_copy = pltpu.make_async_copy(merge_ref, merge_all, merge_sem)
    proj_copy.start()
    merge_copy.start()
    rows, cols, width = own_ref.shape
    lanes = width // 128
    for n in range(lanes):
        part = slice(n * 128, (n + 1) * 128)
        field[n, SHIFT : SHIFT + rows, SHIFT : SHIFT + cols, :] = own_ref[:, :, part].astype(F32)
        field[n, :SHIFT, SHIFT : SHIFT + cols, :] = top_ref[:, :, part].astype(F32)
        field[n, SHIFT + rows :, SHIFT : SHIFT + cols, :] = bottom_ref[:, :, part].astype(F32)
        field[n, :, :SHIFT, :] = left_ref[:, :, part].astype(F32)
        field[n, :, SHIFT + cols :, :] = right_ref[:, :, part].astype(F32)
    across = (cols + WIN) // WIN
    size = WIN * WIN
    low = lax.broadcasted_iota(jnp.int32, (size, 128), 1) < HD
    key_row = lax.broadcasted_iota(jnp.int32, (2 * size, size), 1) // WIN
    first = place_ref[0] * rows - SHIFT
    total = place_ref[1] * rows

    def band(a, carry):
        for b in range(across):
            x = jnp.concatenate(
                [
                    field[n, pl.ds(a * WIN, WIN), b * WIN : (b + 1) * WIN, :].reshape(size, 128)
                    for n in range(lanes)
                ],
                axis=1,
            )
            hold[b * size : (b + 1) * size, :] = normalise(x, gain_attn_ref[...]).astype(BF)
        qkv = jnp.dot(hold[...], qkv_ref[...], preferred_element_type=F32).astype(BF)
        row = first + a * WIN + key_row
        allowed = (row >= 0) & (row < total)
        for b in range(across):
            here = slice(b * size, (b + 1) * size)
            for p in range(lanes):
                q = qkv[here, p * 128 : (p + 1) * 128]
                k = qkv[here, width + p * 128 : width + (p + 1) * 128]
                v = qkv[here, 2 * width + p * 128 : 2 * width + (p + 1) * 128]
                none = jnp.zeros_like(q)
                pair = jnp.concatenate([jnp.where(low, q, none), jnp.where(low, none, q)], axis=0)
                scores = jnp.where(allowed, nt(pair, k) * (1.0 / 8.0), -1e30)
                expo = jnp.exp(scores - jnp.max(scores, axis=1, keepdims=True))
                weights = (expo / jnp.sum(expo, axis=1, keepdims=True)).astype(BF)
                both = jnp.dot(weights, v, preferred_element_type=F32)
                out = jnp.where(low, both[:size], both[size:]).astype(BF).astype(F32)
                att[p, pl.ds(a * WIN, WIN), b * WIN : (b + 1) * WIN, :] = out.reshape(WIN, WIN, 128)
        return carry

    lax.fori_loop(0, (rows + WIN) // WIN, band, 0)

    proj_copy.wait()
    half_rows, half_cols = rows // 2, cols // 2
    tokens = half_rows * half_cols
    pieces = []
    for p in range(4):
        di, dj = p % 2, p // 2
        def pick(ref):
            return jnp.concatenate(
                [
                    jnp.concatenate(
                        [
                            ref[n, SHIFT + di + 2 * i, pl.ds(SHIFT + dj, half_cols, stride=2), :]
                            for i in range(half_rows)
                        ],
                        axis=0,
                    )
                    for n in range(lanes)
                ],
                axis=1,
            )
        got = pick(att).astype(BF)
        att_out[:, p * width : (p + 1) * width] = got
        block = pick(field) + jnp.dot(got, proj_all[...], preferred_element_type=F32)
        block = block.astype(BF)
        merged_out[:, p * width : (p + 1) * width] = block
    merged = merged_out[...].astype(F32)
    merged_norm = normalise(merged, gain_merge_ref[...]).astype(BF)
    for n in range(4):
        pick_out[n] = jnp.concatenate(
            [merged_norm[:, g * 256 + n * 64 : g * 256 + (n + 1) * 64] for g in range(8)], axis=1
        )
    merge_copy.wait()
    coarse = jnp.dot(merged_norm, merge_all[...], preferred_element_type=F32).astype(BF)
    coarse_out[...] = coarse
    norm_out[...] = normalise(coarse.astype(F32), gain_mlp_ref[...]).astype(BF)


def attend(place, own, top, bottom, left, right, gain_attn, w_qkv, w_proj, gain_merge, w_merge, gain_mlp):
    rows, cols, width = own.shape
    tokens = rows * cols // 4
    wide = w_merge.shape[1]
    shapes = [
        jax.ShapeDtypeStruct((tokens, wide), BF),
        jax.ShapeDtypeStruct((tokens, wide), BF),
        jax.ShapeDtypeStruct((tokens, 4 * width), BF),
        jax.ShapeDtypeStruct((4, tokens, width), BF),
        jax.ShapeDtypeStruct((tokens, 4 * width), BF),
    ]
    return pl.pallas_call(
        attend_kernel,
        out_shape=shapes,
        in_specs=[SMEM]
        + [VMEM] * 7
        + [HBM, VMEM, HBM, VMEM],
        out_specs=[VMEM] * 5,
        scratch_shapes=[
            pltpu.VMEM((width // 128, rows + WIN, cols + WIN, 128), F32),
            pltpu.VMEM((width // 128, rows + WIN, cols + WIN, 128), F32),
            pltpu.VMEM(((cols + WIN) * WIN, width), BF),
            pltpu.VMEM(w_proj.shape, BF),
            pltpu.VMEM(w_merge.shape, BF),
            pltpu.SemaphoreType.DMA,
            pltpu.SemaphoreType.DMA,
        ],
        compiler_params=params(),
        cost_estimate=cost(),
    )(place, own, top, bottom, left, right, gain_attn.reshape(1, -1), w_qkv, w_proj, gain_merge.reshape(1, -1), w_merge, gain_mlp.reshape(1, -1))


def hidden_kernel(*refs):
    norms, streams, ups, downs, parts = (refs[i : i + 4] for i in range(0, 20, 4))
    hidden_out, pre_out, norm_all, stream_all, total = refs[20:]
    tokens = norms[0].shape[0]
    chunk = ups[0].shape[1]
    for t in range(4):
        norm_all[t * tokens : (t + 1) * tokens, :] = norms[t][...]
        stream_all[t * tokens : (t + 1) * tokens, :] = streams[t][...]
    for m in range(4):
        up = ups[m][...]
        pre = jnp.dot(norm_all[...], up, preferred_element_type=F32)
        grad_hidden = nt(stream_all[...], downs[m][...])
        tangent = jnp.tanh(0.7978845608 * (pre + 0.044715 * pre * pre * pre))
        hidden = 0.5 * pre * (1.0 + tangent)
        slope = 0.5 * (1.0 + tangent) + 0.5 * pre * (1.0 - tangent * tangent) * 0.7978845608 * (
            1.0 + 3.0 * 0.044715 * pre * pre
        )
        here = slice(m * chunk, (m + 1) * chunk)
        hidden_out[:, here] = hidden.astype(BF)
        grad_pre = (grad_hidden * slope).astype(BF)
        pre_out[:, here] = grad_pre
        part = nt(grad_pre, up)
        if m == 0:
            total[...] = part
        elif m < 3:
            total[...] += part
        else:
            for t in range(4):
                rows = slice(t * tokens, (t + 1) * tokens)
                parts[t][...] = (total[rows, :] + part[rows, :]).astype(BF)


def hidden_units(norms, streams, ups, downs):
    tokens, width = norms[0].shape
    chunk = ups[0].shape[1]
    out = [jax.ShapeDtypeStruct((tokens, width), BF)] * 4
    out += [jax.ShapeDtypeStruct((4 * tokens, 4 * chunk), BF)] * 2
    return pl.pallas_call(
        hidden_kernel,
        out_shape=out,
        in_specs=[VMEM] * 16,
        out_specs=[VMEM] * 6,
        scratch_shapes=[
            pltpu.VMEM((4 * tokens, width), BF),
            pltpu.VMEM((4 * tokens, width), BF),
            pltpu.VMEM((4 * tokens, width), F32),
        ],
        compiler_params=params(),
        cost_estimate=cost(),
    )(*norms, *streams, *ups, *downs)


def weight_grad_kernel(*refs):
    place, norms, streams, hidden, pre = refs[0], refs[1:5], refs[5:9], refs[9], refs[10]
    send, keep, norm_all, stream_all = refs[11:]
    tokens = norms[0].shape[0]
    chunk = pre.shape[1] // 4
    for t in range(4):
        norm_all[t * tokens : (t + 1) * tokens, :] = norms[t][...]
        stream_all[t * tokens : (t + 1) * tokens, :] = streams[t][...]
    for m in (1, 3, 0, 2):
        here = slice(m * chunk, (m + 1) * chunk)
        up = tn(norm_all[...], pre[:, here]).astype(BF)
        down = tn(hidden[:, here], stream_all[...]).astype(BF)
        target = send if m % 2 else keep
        side = lax.rem(place[4] + m // 2, 2)
        for n in range(8):
            block = slice(n * 128, (n + 1) * 128)
            target[n * 2 + side, :128, :] = up[block, :]
            target[n * 2 + side, 128:, :128] = down[:128, block]
            target[n * 2 + side, 128:, 128:] = down[128:, block]


def weight_grads(place, norms, streams, hidden, pre):
    tokens, width = norms[0].shape
    return pl.pallas_call(
        weight_grad_kernel,
        out_shape=[jax.ShapeDtypeStruct((16, 256, 256), BF)] * 2,
        in_specs=[SMEM] + [VMEM] * 10,
        out_specs=[VMEM] * 2,
        scratch_shapes=[pltpu.VMEM((4 * tokens, width), BF), pltpu.VMEM((4 * tokens, width), BF)],
        compiler_params=params(),
        cost_estimate=cost(),
    )(place, *norms, *streams, hidden, pre)


def add(a, b):
    return (a.astype(F32) + b.astype(F32)).astype(BF)


def pair_sum_kernel(keep, got, out):
    out[...] = add(keep[...], got[...])


def all_sum_kernel(blocks, merges, out, merge_out):
    total = blocks[0].astype(F32)
    merge = merges[0].astype(F32)
    for n in range(1, blocks.shape[0]):
        total += blocks[n].astype(F32)
        merge += merges[n].astype(F32)
    for n in range(4):
        merge_out[:, n * 256 : (n + 1) * 256] = merge[n * 16 : (n + 1) * 16, :]
    total = total.astype(BF)
    proj = merge[64:, :].astype(BF)
    for n in range(out.shape[0]):
        out[n, :256, :] = total
        out[n, 256:, :] = proj


def merge_pack_kernel(merge_keep, merge_got, proj_keep, proj_got, out):
    for p in range(out.shape[0]):
        merge = add(merge_keep[p], merge_got[p])
        for n in range(4):
            out[p, n * 16 : (n + 1) * 16, :] = merge[:, n * 256 : (n + 1) * 256]
        out[p, 64:, :] = add(proj_keep[p // 2], proj_got[p // 2])


def sums(kernel, shapes, *args):
    return pl.pallas_call(
        kernel,
        out_shape=[
            jax.ShapeDtypeStruct(shape, F32 if shape == (16, 1024) else BF) for shape in shapes
        ],
        in_specs=[VMEM] * len(args),
        out_specs=[VMEM] * len(shapes),
        compiler_params=params(),
        cost_estimate=cost(),
    )(*args)


def down_kernel(*refs):
    hidden, downs, parts = refs[0], refs[1:5], refs[5:]
    tokens = parts[0].shape[0]
    chunk = downs[0].shape[0]
    for t in range(4):
        rows = slice(t * tokens, (t + 1) * tokens)
        total = 0.0
        for m in range(4):
            total += jnp.dot(
                hidden[rows, m * chunk : (m + 1) * chunk],
                downs[m][...],
                preferred_element_type=F32,
            )
        parts[t][...] = total.astype(BF)


def down_parts(hidden, downs):
    tokens = hidden.shape[0] // 4
    return pl.pallas_call(
        down_kernel,
        out_shape=[jax.ShapeDtypeStruct((tokens, downs[0].shape[1]), BF)] * 4,
        in_specs=[VMEM] * 5,
        out_specs=[VMEM] * 4,
        compiler_params=params(),
        cost_estimate=cost(),
    )(hidden, *downs)


def merge_grad_kernel(place, left, right0, right1, right2, right3, keep, send, both, left_all, right_all):
    tokens, width = left.shape[1:]
    for t, right in enumerate((right0, right1, right2, right3)):
        left_all[t * tokens : (t + 1) * tokens, :] = left[lax.rem(place[2] + 4 - t, 4)]
        right_all[t * tokens : (t + 1) * tokens, :] = right[...]
    part = tn(left_all[...], right_all[...]).astype(BF)
    for n in range(width // 16):
        both[lax.rem(n % 2 + place[5], 2), n // 2] = part[n * 16 : (n + 1) * 16, :]
    keep[...] = both[0]
    send[...] = both[1]


def merge_grads(place, left, rights):
    tokens, width = left.shape[1:]
    last = rights[0].shape[-1]
    return pl.pallas_call(
        merge_grad_kernel,
        out_shape=[jax.ShapeDtypeStruct((width // 32, 16, last), BF)] * 2,
        in_specs=[SMEM] + [VMEM] * 5,
        out_specs=[VMEM] * 2,
        scratch_shapes=[
            pltpu.VMEM((2, width // 32, 16, last), BF),
            pltpu.VMEM((4 * tokens, width), BF),
            pltpu.VMEM((4 * tokens, last), BF),
        ],
        compiler_params=params(),
        cost_estimate=cost(),
    )(place, left, *rights)


def place_kernel(blocks, up, down):
    for n in range(8):
        block = slice(n * 128, (n + 1) * 128)
        up[block, :] = blocks[n, :128, :].astype(F32)
        down[:128, block] = blocks[n, 128:256, :128].astype(F32)
        down[128:, block] = blocks[n, 128:256, 128:].astype(F32)


def place_blocks(blocks):
    return pl.pallas_call(
        place_kernel,
        out_shape=[
            jax.ShapeDtypeStruct((1024, 256), F32),
            jax.ShapeDtypeStruct((256, 1024), F32),
        ],
        in_specs=[VMEM],
        out_specs=[VMEM] * 2,
        compiler_params=params(),
        cost_estimate=cost(),
    )(blocks)


def proj_kernel(place, own, other, out):
    for k in range(4):
        y = lax.rem(place[2] + 4 - k, 4)
        for side, ref in enumerate((own, other)):
            c = lax.rem(place[5] + side, 2)
            for n in range(8):
                start = pl.multiple_of((y * 16 + c * 8 + n) * 8, 8)
                block = ref[k, n].astype(F32)
                out[pl.ds(start, 8), :256] = block[:8, :]
                out[pl.ds(start, 8), 256:] = block[8:, :]


def place_proj(place, own, other):
    return pl.pallas_call(
        proj_kernel,
        out_shape=jax.ShapeDtypeStruct((512, 512), F32),
        in_specs=[SMEM] + [VMEM] * 2,
        out_specs=VMEM,
        compiler_params=params(),
        cost_estimate=cost(),
    )(place, own, other)


def norm_back(values, gain, upstream):
    center = values - jnp.mean(values, axis=-1, keepdims=True)
    spread = jnp.mean(center * center, axis=-1, keepdims=True)
    factor = lax.rsqrt(spread + 1e-05)
    normal = center * factor
    scaled = upstream * gain
    return factor * (
        scaled
        - jnp.mean(scaled, axis=-1, keepdims=True)
        - normal * jnp.mean(scaled * normal, axis=-1, keepdims=True)
    )


def skip_kernel(
    place, coarse_grad, gain, merge, merged, att, skip, proj0, proj1, proj2, proj3, hold, blocks
):
    lanes = hold.shape[0]
    width = lanes * 128
    half_rows, half_cols = hold.shape[1] // 2, hold.shape[2] // 2
    grad = nt(coarse_grad[...], merge[...])
    grad = norm_back(merged[...].astype(F32), gain[...], grad).astype(BF)
    total = None
    for p in range(4):
        di, dj = p % 2, p // 2
        piece = grad[:, p * width : (p + 1) * width]
        part = tn(att[:, p * width : (p + 1) * width], piece)
        total = part if total is None else total + part
        wide = piece.astype(F32)
        for n in range(lanes):
            for i in range(half_rows):
                hold[n, di + 2 * i, pl.ds(dj, half_cols, stride=2), :] = wide[
                    i * half_cols : (i + 1) * half_cols, n * 128 : (n + 1) * 128
                ]
    for n in range(lanes):
        skip[:, :, n * 128 : (n + 1) * 128] = hold[n].astype(BF)
    for n in range(width // 8):
        dy = lax.rem(n // 16 + 4 - place[2], 4)
        dc = lax.rem(n // 8 % 2 + place[5], 2)
        rows = slice(n * 8, (n + 1) * 8)
        block = jnp.concatenate([total[rows, : width // 2], total[rows, width // 2 :]], axis=0)
        blocks[dy, dc, n % 8] = block.astype(BF)
    for n, out in enumerate((proj0, proj1, proj2, proj3)):
        out[...] = blocks[n]


def skip_grads(place, coarse_grad, gain, merge, merged, att, rows, cols):
    width = att.shape[1] // 4
    return pl.pallas_call(
        skip_kernel,
        out_shape=[
            jax.ShapeDtypeStruct((rows, cols, width), BF),
        ]
        + [jax.ShapeDtypeStruct((2, 8, 16, width // 2), BF)] * 4,
        in_specs=[SMEM] + [VMEM] * 5,
        out_specs=[VMEM] * 5,
        scratch_shapes=[
            pltpu.VMEM((width // 128, rows, cols, 128), F32),
            pltpu.VMEM((4, 2, 8, 16, width // 2), BF),
        ],
        compiler_params=params(),
        cost_estimate=cost(),
    )(place, coarse_grad, gain.reshape(1, -1), merge, merged, att)


def per_device(
    level_one, gain_attn, w_qkv, w_proj, gain_merge, w_merge, gain_mlp, w_up, w_down, cotangent
):
    tile_rows, tile_cols, feature = level_one.shape
    width = cotangent.shape[-1]
    upstream = cotangent.reshape(-1, width)
    place = jnp.stack(
        [lax.axis_index(LAT), jnp.int32(lax.axis_size(LAT))]
        + [lax.axis_index(name) for name in ("y", "z", "xl", "c", "xh")]
    ).astype(jnp.int32)

    top = rotate(level_one[-SHIFT:], LAT, 1)
    bottom = rotate(level_one[:SHIFT], LAT, -1)
    top, bottom = together(top, bottom)

    tall = [top, level_one, bottom]
    left = rotate(jnp.concatenate([part[:, -SHIFT:] for part in tall], axis=0), LON, 1)
    right = rotate(jnp.concatenate([part[:, :SHIFT] for part in tall], axis=0), LON, -1)
    left, right, first_up, first_down, upstream = together(
        left, right, w_up, w_down, upstream
    )

    coarse_norm, coarse, merged, picks, att = attend(
        place, level_one, top, bottom, left, right, gain_attn, w_qkv, w_proj,
        gain_merge, w_merge, gain_mlp,
    )
    up_x, up_c = rotate(first_up, "xl", 1), rotate(first_up, "c", 1)
    streams = gather_rel(upstream, "y")
    coarse_norm, picks, up_x, up_c, streams, first_down = together(
        coarse_norm, picks, up_x, up_c, streams, first_down
    )

    down_x, up_xc = rotate(first_down, "xl", 1), rotate(up_x, "c", 1)
    norms = gather_rel(coarse_norm, "y")
    norms, up_xc, down_x, picks, first_down = together(norms, up_xc, down_x, picks, first_down)

    down_c, down_xc = rotate(first_down, "c", 1), rotate(down_x, "c", 1)
    lefts = lax.all_to_all(picks, "y", 0, 0)
    ups, downs = [w_up, up_c, up_x, up_xc], [w_down, down_c, down_x, down_xc]
    *parts, hidden, grad_pre = hidden_units(norms, streams, ups, downs)
    parts, hidden, grad_pre, lefts = together(parts, hidden, grad_pre, lefts)

    arrived = [rotate(parts[k], "y", -k) for k in range(1, 4)]
    send, keep = weight_grads(place, norms, streams, hidden, grad_pre)
    (blocks,) = sums(pair_sum_kernel, [(16, 256, 256)], keep, rotate(send, "c", 1))
    outer = down_parts(hidden, downs)
    arrived, outer = together(arrived, outer)
    grad_norm = sum(part.astype(F32) for part in [parts[0]] + arrived)
    grad_coarse = (
        upstream.astype(F32) + norm_back(coarse.astype(F32), gain_mlp, grad_norm)
    ).astype(BF)

    blocks = lax.all_to_all(blocks, LAT + ("xl",), 0, 0)
    rights = gather_rel(grad_coarse, "y")
    grad_skip, *projs = skip_grads(
        place, grad_coarse, gain_merge, w_merge, merged, att, tile_rows, tile_cols
    )
    rights, grad_skip = together(rights, grad_skip)
    proj = sum(
        part.astype(F32)
        for part in [projs[0]] + [rotate(projs[k], "y", k) for k in range(1, 4)]
    ).astype(BF)
    proj_got = rotate(proj[1], "c", 1)
    merge_keep, merge_send = merge_grads(place, lefts, rights)
    merge_got = rotate(merge_send, "c", 1)
    (merges,) = sums(
        merge_pack_kernel, [(16, 80, 256)], merge_keep, merge_got, proj[0], proj_got
    )
    blocks, merges, outer = together(blocks, merges, outer)

    merges = lax.all_to_all(merges, LAT + ("xl",), 0, 0)
    merges, outer = together(merges, outer)

    blocks, grad_merge = sums(all_sum_kernel, [(8, 272, 256), (16, 1024)], blocks, merges)
    blocks = lax.all_to_all(blocks, LAT, 0, 0)
    summed = scatter_rel(outer, "y", -1)
    level_two = (coarse.astype(F32) + summed).astype(BF)
    blocks, level_two = together(blocks, level_two)

    proj = jnp.stack(gather_rel(blocks[:, 256:], "y"))
    grad_up, grad_down = place_blocks(blocks)
    proj, grad_up = together(proj, grad_up)
    grad_proj = place_proj(place, proj, rotate(proj, "c", 1))

    level_two = level_two.reshape(tile_rows // 2, tile_cols // 2, width)
    return (level_two, grad_skip, grad_proj, grad_merge, grad_up, grad_down)


def solution(mesh):
    fine = Mesh(mesh.devices.reshape(2, 4, 4, 2, 2), LAT + LON)
    grid = P(LAT, LON, None)
    placed = (grid, P(), P(), P(), P(), P(), P(), P(None, LON), P(LON, None), grid)
    return jax.shard_map(
        per_device,
        mesh=fine,
        in_specs=placed,
        out_specs=(grid, grid, P(), P(LAT + LON, None), P(None, LON), P(LON, None)),
        check_vma=False,
    )
```

```python
import jax
import jax.numpy as jnp
from jax import lax
from jax.experimental import pallas as pl
from jax.experimental.pallas import tpu as pltpu
from jax.sharding import Mesh
from jax.sharding import PartitionSpec as P

HD = 64
WIN = 8
SHIFT = 4
LAT = ("xh", "z")
LON = ("y", "xl", "c")
F32 = jnp.float32
BF = jnp.bfloat16
VMEM = pl.BlockSpec(memory_space=pltpu.VMEM)
HBM = pl.BlockSpec(memory_space=pl.ANY)
SMEM = pl.BlockSpec(memory_space=pltpu.SMEM)


def rotate(value, axis, shift):
    size = lax.axis_size(axis)
    return lax.ppermute(value, axis, [(i, (i + shift) % size) for i in range(size)])


def params():
    return pltpu.CompilerParams(vmem_limit_bytes=62 * 2**20)


def cost():
    return pl.CostEstimate(flops=1000, bytes_accessed=1000, transcendentals=0)


def together(*values):
    return lax.optimization_barrier(values)


def scatter_rel(parts, axis, way):
    total = parts[0].astype(F32)
    for k in range(1, len(parts)):
        total = total + rotate(parts[k], axis, way * k).astype(F32)
    return total


def gather_rel(value, axis):
    return [value] + [rotate(value, axis, k) for k in range(1, lax.axis_size(axis))]


def normalise(values, gain):
    center = values - jnp.mean(values, axis=-1, keepdims=True)
    spread = jnp.mean(center * center, axis=-1, keepdims=True)
    return center * lax.rsqrt(spread + 1e-05) * gain


def nt(a, b):
    return lax.dot_general(a, b, (((1,), (1,)), ((), ())), preferred_element_type=F32)


def tn(a, b):
    return lax.dot_general(a, b, (((0,), (0,)), ((), ())), preferred_element_type=F32)


def attend_kernel(
    place_ref, own_ref, top_ref, bottom_ref, left_ref, right_ref, gain_attn_ref, qkv_ref, proj_ref,
    gain_merge_ref, merge_ref, gain_mlp_ref,
    norm_out, coarse_out, merged_out, pick_out, att_out,
    field, att, hold, proj_all, merge_all, proj_sem, merge_sem,
):
    proj_copy = pltpu.make_async_copy(proj_ref, proj_all, proj_sem)
    merge_copy = pltpu.make_async_copy(merge_ref, merge_all, merge_sem)
    proj_copy.start()
    merge_copy.start()
    rows, cols, width = own_ref.shape
    lanes = width // 128
    for n in range(lanes):
        part = slice(n * 128, (n + 1) * 128)
        field[n, SHIFT : SHIFT + rows, SHIFT : SHIFT + cols, :] = own_ref[:, :, part].astype(F32)
        field[n, :SHIFT, SHIFT : SHIFT + cols, :] = top_ref[:, :, part].astype(F32)
        field[n, SHIFT + rows :, SHIFT : SHIFT + cols, :] = bottom_ref[:, :, part].astype(F32)
        field[n, :, :SHIFT, :] = left_ref[:, :, part].astype(F32)
        field[n, :, SHIFT + cols :, :] = right_ref[:, :, part].astype(F32)
    across = (cols + WIN) // WIN
    size = WIN * WIN
    low = lax.broadcasted_iota(jnp.int32, (size, 128), 1) < HD
    key_row = lax.broadcasted_iota(jnp.int32, (2 * size, size), 1) // WIN
    first = place_ref[0] * rows - SHIFT
    total = place_ref[1] * rows

    def band(a, carry):
        for b in range(across):
            x = jnp.concatenate(
                [
                    field[n, pl.ds(a * WIN, WIN), b * WIN : (b + 1) * WIN, :].reshape(size, 128)
                    for n in range(lanes)
                ],
                axis=1,
            )
            hold[b * size : (b + 1) * size, :] = normalise(x, gain_attn_ref[...]).astype(BF)
        qkv = jnp.dot(hold[...], qkv_ref[...], preferred_element_type=F32).astype(BF)
        row = first + a * WIN + key_row
        allowed = (row >= 0) & (row < total)
        for b in range(across):
            here = slice(b * size, (b + 1) * size)
            for p in range(lanes):
                q = qkv[here, p * 128 : (p + 1) * 128]
                k = qkv[here, width + p * 128 : width + (p + 1) * 128]
                v = qkv[here, 2 * width + p * 128 : 2 * width + (p + 1) * 128]
                none = jnp.zeros_like(q)
                pair = jnp.concatenate([jnp.where(low, q, none), jnp.where(low, none, q)], axis=0)
                scores = jnp.where(allowed, nt(pair, k) * (1.0 / 8.0), -1e30)
                expo = jnp.exp(scores - jnp.max(scores, axis=1, keepdims=True))
                weights = (expo / jnp.sum(expo, axis=1, keepdims=True)).astype(BF)
                both = jnp.dot(weights, v, preferred_element_type=F32)
                out = jnp.where(low, both[:size], both[size:]).astype(BF).astype(F32)
                att[p, pl.ds(a * WIN, WIN), b * WIN : (b + 1) * WIN, :] = out.reshape(WIN, WIN, 128)
        return carry

    lax.fori_loop(0, (rows + WIN) // WIN, band, 0)

    proj_copy.wait()
    half_rows, half_cols = rows // 2, cols // 2
    tokens = half_rows * half_cols
    pieces = []
    for p in range(4):
        di, dj = p % 2, p // 2
        def pick(ref):
            return jnp.concatenate(
                [
                    jnp.concatenate(
                        [
                            ref[n, SHIFT + di + 2 * i, pl.ds(SHIFT + dj, half_cols, stride=2), :]
                            for i in range(half_rows)
                        ],
                        axis=0,
                    )
                    for n in range(lanes)
                ],
                axis=1,
            )
        got = pick(att).astype(BF)
        att_out[:, p * width : (p + 1) * width] = got
        block = pick(field) + jnp.dot(got, proj_all[...], preferred_element_type=F32)
        block = block.astype(BF)
        merged_out[:, p * width : (p + 1) * width] = block
    merged = merged_out[...].astype(F32)
    merged_norm = normalise(merged, gain_merge_ref[...]).astype(BF)
    for n in range(4):
        pick_out[n] = jnp.concatenate(
            [merged_norm[:, g * 256 + n * 64 : g * 256 + (n + 1) * 64] for g in range(8)], axis=1
        )
    merge_copy.wait()
    coarse = jnp.dot(merged_norm, merge_all[...], preferred_element_type=F32).astype(BF)
    coarse_out[...] = coarse
    norm_out[...] = normalise(coarse.astype(F32), gain_mlp_ref[...]).astype(BF)


def attend(place, own, top, bottom, left, right, gain_attn, w_qkv, w_proj, gain_merge, w_merge, gain_mlp):
    rows, cols, width = own.shape
    tokens = rows * cols // 4
    wide = w_merge.shape[1]
    shapes = [
        jax.ShapeDtypeStruct((tokens, wide), BF),
        jax.ShapeDtypeStruct((tokens, wide), BF),
        jax.ShapeDtypeStruct((tokens, 4 * width), BF),
        jax.ShapeDtypeStruct((4, tokens, width), BF),
        jax.ShapeDtypeStruct((tokens, 4 * width), BF),
    ]
    return pl.pallas_call(
        attend_kernel,
        out_shape=shapes,
        in_specs=[SMEM]
        + [VMEM] * 7
        + [HBM, VMEM, HBM, VMEM],
        out_specs=[VMEM] * 5,
        scratch_shapes=[
            pltpu.VMEM((width // 128, rows + WIN, cols + WIN, 128), F32),
            pltpu.VMEM((width // 128, rows + WIN, cols + WIN, 128), F32),
            pltpu.VMEM(((cols + WIN) * WIN, width), BF),
            pltpu.VMEM(w_proj.shape, BF),
            pltpu.VMEM(w_merge.shape, BF),
            pltpu.SemaphoreType.DMA,
            pltpu.SemaphoreType.DMA,
        ],
        compiler_params=params(),
        cost_estimate=cost(),
    )(place, own, top, bottom, left, right, gain_attn.reshape(1, -1), w_qkv, w_proj, gain_merge.reshape(1, -1), w_merge, gain_mlp.reshape(1, -1))


def hidden_kernel(*refs):
    norms, streams, ups, downs, parts = (refs[i : i + 4] for i in range(0, 20, 4))
    hidden_out, pre_out, norm_all, stream_all, total = refs[20:]
    tokens = norms[0].shape[0]
    chunk = ups[0].shape[1]
    for t in range(4):
        norm_all[t * tokens : (t + 1) * tokens, :] = norms[t][...]
        stream_all[t * tokens : (t + 1) * tokens, :] = streams[t][...]
    for m in range(4):
        up = ups[m][...]
        pre = jnp.dot(norm_all[...], up, preferred_element_type=F32)
        grad_hidden = nt(stream_all[...], downs[m][...])
        tangent = jnp.tanh(0.7978845608 * (pre + 0.044715 * pre * pre * pre))
        hidden = 0.5 * pre * (1.0 + tangent)
        slope = 0.5 * (1.0 + tangent) + 0.5 * pre * (1.0 - tangent * tangent) * 0.7978845608 * (
            1.0 + 3.0 * 0.044715 * pre * pre
        )
        here = slice(m * chunk, (m + 1) * chunk)
        hidden_out[:, here] = hidden.astype(BF)
        grad_pre = (grad_hidden * slope).astype(BF)
        pre_out[:, here] = grad_pre
        part = nt(grad_pre, up)
        if m == 0:
            total[...] = part
        elif m < 3:
            total[...] += part
        else:
            for t in range(4):
                rows = slice(t * tokens, (t + 1) * tokens)
                parts[t][...] = (total[rows, :] + part[rows, :]).astype(BF)


def hidden_units(norms, streams, ups, downs):
    tokens, width = norms[0].shape
    chunk = ups[0].shape[1]
    out = [jax.ShapeDtypeStruct((tokens, width), BF)] * 4
    out += [jax.ShapeDtypeStruct((4 * tokens, 4 * chunk), BF)] * 2
    return pl.pallas_call(
        hidden_kernel,
        out_shape=out,
        in_specs=[VMEM] * 16,
        out_specs=[VMEM] * 6,
        scratch_shapes=[
            pltpu.VMEM((4 * tokens, width), BF),
            pltpu.VMEM((4 * tokens, width), BF),
            pltpu.VMEM((4 * tokens, width), F32),
        ],
        compiler_params=params(),
        cost_estimate=cost(),
    )(*norms, *streams, *ups, *downs)


def weight_grad_kernel(*refs):
    place, norms, streams, hidden, pre = refs[0], refs[1:5], refs[5:9], refs[9], refs[10]
    send, keep, norm_all, stream_all = refs[11:]
    tokens = norms[0].shape[0]
    chunk = pre.shape[1] // 4
    for t in range(4):
        norm_all[t * tokens : (t + 1) * tokens, :] = norms[t][...]
        stream_all[t * tokens : (t + 1) * tokens, :] = streams[t][...]
    for m in (1, 3, 0, 2):
        here = slice(m * chunk, (m + 1) * chunk)
        up = tn(norm_all[...], pre[:, here]).astype(BF)
        down = tn(hidden[:, here], stream_all[...]).astype(BF)
        target = send if m % 2 else keep
        side = lax.rem(place[4] + m // 2, 2)
        for n in range(8):
            block = slice(n * 128, (n + 1) * 128)
            target[n * 2 + side, :128, :] = up[block, :]
            target[n * 2 + side, 128:, :128] = down[:128, block]
            target[n * 2 + side, 128:, 128:] = down[128:, block]


def weight_grads(place, norms, streams, hidden, pre):
    tokens, width = norms[0].shape
    return pl.pallas_call(
        weight_grad_kernel,
        out_shape=[jax.ShapeDtypeStruct((16, 256, 256), BF)] * 2,
        in_specs=[SMEM] + [VMEM] * 10,
        out_specs=[VMEM] * 2,
        scratch_shapes=[pltpu.VMEM((4 * tokens, width), BF), pltpu.VMEM((4 * tokens, width), BF)],
        compiler_params=params(),
        cost_estimate=cost(),
    )(place, *norms, *streams, hidden, pre)


def add(a, b):
    return (a.astype(F32) + b.astype(F32)).astype(BF)


def pair_sum_kernel(keep, got, out):
    out[...] = add(keep[...], got[...])


def block_sum_kernel(blocks, out):
    total = blocks[0].astype(F32)
    for n in range(1, blocks.shape[0]):
        total += blocks[n].astype(F32)
    out[...] = total.astype(BF)


def all_sum_kernel(total, merges, out, merge_out):
    merge = merges[0].astype(F32)
    for n in range(1, merges.shape[0]):
        merge += merges[n].astype(F32)
    for n in range(4):
        merge_out[:, n * 256 : (n + 1) * 256] = merge[n * 16 : (n + 1) * 16, :]
    proj = merge[64:, :].astype(BF)
    for n in range(out.shape[0]):
        out[n, :256, :] = total[...]
        out[n, 256:, :] = proj


def merge_pack_kernel(merge_keep, merge_got, proj_keep, proj_got, out):
    for p in range(out.shape[0]):
        merge = add(merge_keep[p], merge_got[p])
        for n in range(4):
            out[p, n * 16 : (n + 1) * 16, :] = merge[:, n * 256 : (n + 1) * 256]
        out[p, 64:, :] = add(proj_keep[p // 2], proj_got[p // 2])


def sums(kernel, shapes, *args):
    return pl.pallas_call(
        kernel,
        out_shape=[
            jax.ShapeDtypeStruct(shape, F32 if shape == (16, 1024) else BF) for shape in shapes
        ],
        in_specs=[VMEM] * len(args),
        out_specs=[VMEM] * len(shapes),
        compiler_params=params(),
        cost_estimate=cost(),
    )(*args)


def down_kernel(*refs):
    hidden, downs, parts = refs[0], refs[1:5], refs[5:]
    tokens = parts[0].shape[0]
    chunk = downs[0].shape[0]
    for t in range(4):
        rows = slice(t * tokens, (t + 1) * tokens)
        total = 0.0
        for m in range(4):
            total += jnp.dot(
                hidden[rows, m * chunk : (m + 1) * chunk],
                downs[m][...],
                preferred_element_type=F32,
            )
        parts[t][...] = total.astype(BF)


def down_parts(hidden, downs):
    tokens = hidden.shape[0] // 4
    return pl.pallas_call(
        down_kernel,
        out_shape=[jax.ShapeDtypeStruct((tokens, downs[0].shape[1]), BF)] * 4,
        in_specs=[VMEM] * 5,
        out_specs=[VMEM] * 4,
        compiler_params=params(),
        cost_estimate=cost(),
    )(hidden, *downs)


def merge_grad_kernel(place, left, right0, right1, right2, right3, keep, send, both, left_all, right_all):
    tokens, width = left.shape[1:]
    for t, right in enumerate((right0, right1, right2, right3)):
        left_all[t * tokens : (t + 1) * tokens, :] = left[lax.rem(place[2] + 4 - t, 4)]
        right_all[t * tokens : (t + 1) * tokens, :] = right[...]
    part = tn(left_all[...], right_all[...]).astype(BF)
    for n in range(width // 16):
        both[lax.rem(n % 2 + place[5], 2), n // 2] = part[n * 16 : (n + 1) * 16, :]
    keep[...] = both[0]
    send[...] = both[1]


def merge_grads(place, left, rights):
    tokens, width = left.shape[1:]
    last = rights[0].shape[-1]
    return pl.pallas_call(
        merge_grad_kernel,
        out_shape=[jax.ShapeDtypeStruct((width // 32, 16, last), BF)] * 2,
        in_specs=[SMEM] + [VMEM] * 5,
        out_specs=[VMEM] * 2,
        scratch_shapes=[
            pltpu.VMEM((2, width // 32, 16, last), BF),
            pltpu.VMEM((4 * tokens, width), BF),
            pltpu.VMEM((4 * tokens, last), BF),
        ],
        compiler_params=params(),
        cost_estimate=cost(),
    )(place, left, *rights)


def place_kernel(blocks, up, down):
    for n in range(8):
        block = slice(n * 128, (n + 1) * 128)
        up[block, :] = blocks[n, :128, :].astype(F32)
        down[:128, block] = blocks[n, 128:256, :128].astype(F32)
        down[128:, block] = blocks[n, 128:256, 128:].astype(F32)


def place_blocks(blocks):
    return pl.pallas_call(
        place_kernel,
        out_shape=[
            jax.ShapeDtypeStruct((1024, 256), F32),
            jax.ShapeDtypeStruct((256, 1024), F32),
        ],
        in_specs=[VMEM],
        out_specs=[VMEM] * 2,
        compiler_params=params(),
        cost_estimate=cost(),
    )(blocks)


def proj_kernel(place, own, other, out):
    for k in range(4):
        y = lax.rem(place[2] + 4 - k, 4)
        for side, ref in enumerate((own, other)):
            c = lax.rem(place[5] + side, 2)
            for n in range(8):
                start = pl.multiple_of((y * 16 + c * 8 + n) * 8, 8)
                block = ref[k, n].astype(F32)
                out[pl.ds(start, 8), :256] = block[:8, :]
                out[pl.ds(start, 8), 256:] = block[8:, :]


def place_proj(place, own, other):
    return pl.pallas_call(
        proj_kernel,
        out_shape=jax.ShapeDtypeStruct((512, 512), F32),
        in_specs=[SMEM] + [VMEM] * 2,
        out_specs=VMEM,
        compiler_params=params(),
        cost_estimate=cost(),
    )(place, own, other)


def norm_back(values, gain, upstream):
    center = values - jnp.mean(values, axis=-1, keepdims=True)
    spread = jnp.mean(center * center, axis=-1, keepdims=True)
    factor = lax.rsqrt(spread + 1e-05)
    normal = center * factor
    scaled = upstream * gain
    return factor * (
        scaled
        - jnp.mean(scaled, axis=-1, keepdims=True)
        - normal * jnp.mean(scaled * normal, axis=-1, keepdims=True)
    )


def skip_kernel(
    place, coarse_grad, gain, merge, merged, att, skip, proj0, proj1, proj2, proj3, hold, blocks
):
    lanes = hold.shape[0]
    width = lanes * 128
    half_rows, half_cols = hold.shape[1] // 2, hold.shape[2] // 2
    grad = nt(coarse_grad[...], merge[...])
    grad = norm_back(merged[...].astype(F32), gain[...], grad).astype(BF)
    total = None
    for p in range(4):
        di, dj = p % 2, p // 2
        piece = grad[:, p * width : (p + 1) * width]
        part = tn(att[:, p * width : (p + 1) * width], piece)
        total = part if total is None else total + part
        wide = piece.astype(F32)
        for n in range(lanes):
            for i in range(half_rows):
                hold[n, di + 2 * i, pl.ds(dj, half_cols, stride=2), :] = wide[
                    i * half_cols : (i + 1) * half_cols, n * 128 : (n + 1) * 128
                ]
    for n in range(lanes):
        skip[:, :, n * 128 : (n + 1) * 128] = hold[n].astype(BF)
    for n in range(width // 8):
        dy = lax.rem(n // 16 + 4 - place[2], 4)
        dc = lax.rem(n // 8 % 2 + place[5], 2)
        rows = slice(n * 8, (n + 1) * 8)
        block = jnp.concatenate([total[rows, : width // 2], total[rows, width // 2 :]], axis=0)
        blocks[dy, dc, n % 8] = block.astype(BF)
    for n, out in enumerate((proj0, proj1, proj2, proj3)):
        out[...] = blocks[n]


def skip_grads(place, coarse_grad, gain, merge, merged, att, rows, cols):
    width = att.shape[1] // 4
    return pl.pallas_call(
        skip_kernel,
        out_shape=[
            jax.ShapeDtypeStruct((rows, cols, width), BF),
        ]
        + [jax.ShapeDtypeStruct((2, 8, 16, width // 2), BF)] * 4,
        in_specs=[SMEM] + [VMEM] * 5,
        out_specs=[VMEM] * 5,
        scratch_shapes=[
            pltpu.VMEM((width // 128, rows, cols, 128), F32),
            pltpu.VMEM((4, 2, 8, 16, width // 2), BF),
        ],
        compiler_params=params(),
        cost_estimate=cost(),
    )(place, coarse_grad, gain.reshape(1, -1), merge, merged, att)


def per_device(
    level_one, gain_attn, w_qkv, w_proj, gain_merge, w_merge, gain_mlp, w_up, w_down, cotangent
):
    tile_rows, tile_cols, feature = level_one.shape
    width = cotangent.shape[-1]
    upstream = cotangent.reshape(-1, width)
    place = jnp.stack(
        [lax.axis_index(LAT), jnp.int32(lax.axis_size(LAT))]
        + [lax.axis_index(name) for name in ("y", "z", "xl", "c", "xh")]
    ).astype(jnp.int32)

    top = rotate(level_one[-SHIFT:], LAT, 1)
    bottom = rotate(level_one[:SHIFT], LAT, -1)
    top, bottom = together(top, bottom)

    tall = [top, level_one, bottom]
    left = rotate(jnp.concatenate([part[:, -SHIFT:] for part in tall], axis=0), LON, 1)
    right = rotate(jnp.concatenate([part[:, :SHIFT] for part in tall], axis=0), LON, -1)
    left, right, first_up, first_down, upstream = together(
        left, right, w_up, w_down, upstream
    )

    coarse_norm, coarse, merged, picks, att = attend(
        place, level_one, top, bottom, left, right, gain_attn, w_qkv, w_proj,
        gain_merge, w_merge, gain_mlp,
    )
    up_x, up_c = rotate(first_up, "xl", 1), rotate(first_up, "c", 1)
    streams = gather_rel(upstream, "y")
    coarse_norm, picks, up_x, up_c, streams, first_down = together(
        coarse_norm, picks, up_x, up_c, streams, first_down
    )

    down_x, up_xc = rotate(first_down, "xl", 1), rotate(up_x, "c", 1)
    norms = gather_rel(coarse_norm, "y")
    norms, up_xc, down_x, picks, first_down = together(norms, up_xc, down_x, picks, first_down)

    down_c, down_xc = rotate(first_down, "c", 1), rotate(down_x, "c", 1)
    lefts = lax.all_to_all(picks, "y", 0, 0)
    ups, downs = [w_up, up_c, up_x, up_xc], [w_down, down_c, down_x, down_xc]
    *parts, hidden, grad_pre = hidden_units(norms, streams, ups, downs)
    parts, hidden, grad_pre, lefts = together(parts, hidden, grad_pre, lefts)

    arrived = [rotate(parts[k], "y", -k) for k in range(1, 4)]
    send, keep = weight_grads(place, norms, streams, hidden, grad_pre)
    (blocks,) = sums(pair_sum_kernel, [(16, 256, 256)], keep, rotate(send, "c", 1))
    outer = down_parts(hidden, downs)
    arrived, outer = together(arrived, outer)
    grad_norm = sum(part.astype(F32) for part in [parts[0]] + arrived)
    grad_coarse = (
        upstream.astype(F32) + norm_back(coarse.astype(F32), gain_mlp, grad_norm)
    ).astype(BF)

    blocks = lax.all_to_all(blocks, LAT + ("xl",), 0, 0)
    rights = gather_rel(grad_coarse, "y")
    grad_skip, *projs = skip_grads(
        place, grad_coarse, gain_merge, w_merge, merged, att, tile_rows, tile_cols
    )
    rights, grad_skip = together(rights, grad_skip)
    proj = sum(
        part.astype(F32)
        for part in [projs[0]] + [rotate(projs[k], "y", k) for k in range(1, 4)]
    ).astype(BF)
    proj_got = rotate(proj[1], "c", 1)
    merge_keep, merge_send = merge_grads(place, lefts, rights)
    merge_got = rotate(merge_send, "c", 1)
    (merges,) = sums(
        merge_pack_kernel, [(16, 80, 256)], merge_keep, merge_got, proj[0], proj_got
    )
    blocks, merges, outer = together(blocks, merges, outer)

    merges = lax.all_to_all(merges, LAT + ("xl",), 0, 0)
    (total,) = sums(block_sum_kernel, [(256, 256)], blocks)
    merges, outer, total = together(merges, outer, total)

    blocks, grad_merge = sums(all_sum_kernel, [(8, 272, 256), (16, 1024)], total, merges)
    blocks = lax.all_to_all(blocks, LAT, 0, 0)
    summed = scatter_rel(outer, "y", -1)
    level_two = (coarse.astype(F32) + summed).astype(BF)
    blocks, level_two = together(blocks, level_two)

    proj = jnp.stack(gather_rel(blocks[:, 256:], "y"))
    grad_up, grad_down = place_blocks(blocks)
    proj, grad_up = together(proj, grad_up)
    grad_proj = place_proj(place, proj, rotate(proj, "c", 1))

    level_two = level_two.reshape(tile_rows // 2, tile_cols // 2, width)
    return (level_two, grad_skip, grad_proj, grad_merge, grad_up, grad_down)


def solution(mesh):
    fine = Mesh(mesh.devices.reshape(2, 4, 4, 2, 2), LAT + LON)
    grid = P(LAT, LON, None)
    placed = (grid, P(), P(), P(), P(), P(), P(), P(None, LON), P(LON, None), grid)
    return jax.shard_map(
        per_device,
        mesh=fine,
        in_specs=placed,
        out_specs=(grid, grid, P(), P(LAT + LON, None), P(None, LON), P(LON, None)),
        check_vma=False,
    )
```
